32 devices in a mesh: groups: 2 (over y), frame: 4 (over z), row: 2 (over x), col: 2 (over core).
Axes of the slice: x: 2, y: 2, z: 4, core: 2. Of those that a mesh axis runs over, the one named last changes fastest.
Arguments:
- raw: float32 [8, 256, 512], P(('groups', 'frame'), 'row', 'col'), parts along dimension 0, may hold values from 0.5 to 6.5
- dark: float32 [256, 512], P('row', 'col'), may hold values from 0 to 0.3
- gain: float32 [256, 512], P('row', 'col'), may hold values from 0.5 to 1.5
- bad: int32 [256, 512], P('row', 'col'), may hold values from 0 to 1, as said below
- taps_col: float32 [31], replicated, may hold values from 0.015 to 0.05
- taps_row: float32 [31], replicated, may hold values from 0.015 to 0.05
- levels: int32 [8, 4, 8, 32], P(('groups', 'frame'), 'row', 'col'), parts along dimension 0, may hold values from 0 to 15
- level_table: float32 [16], replicated, may hold values from -0.6 to 0.6
- basis: float32 [32, 4096], replicated, may hold values from -4 to 4
- apod_index: int32 [4, 8], P('row', 'col'), may hold values from 0 to 7
- window_table: float32 [8, 128], replicated, may hold values from 0.2 to 1
- noise: float32 [128, 128], replicated, may hold values from 0.05 to 0.5
Outputs:
- restored: float32 [512, 2, 256], P(('groups', 'row'), 'col', 'frame'), parts along dimension 0
The draws below stay inside these ranges and needn't reach their ends.
There are 2 independent parts, one for each index of `groups`. The reference program is written for one: setup_inputs(seed, part) draws one part's arguments, and reference() takes and returns one part's arrays. A program takes and returns all parts, laid end to end along the dimension named above; an argument that names none is the same for every part. Nothing has to cross between parts.
Inputs may be any that keep to these rules, and one draw needn't show every extreme that they name: A bad pixel lies only in a column whose index is one more than a multiple of 4.
All inputs are finite; a program needn't handle non-finite values.
Results may differ from the reference program's by a relative error of at most 0.0003.
Values sent between devices are 32-bit elements; how exact they have to be, the bound alone decides.
A program may use at most 128 MiB of HBM per device.

```python
import math
import jax
import jax.numpy as jnp
from jax import lax

PATCH = 128
PUPIL = 64
MODES = 32
LEVELS = 16
TAPS = 31
WINDOWS = 8
FRAMES = 4
GRID_R = 4
GRID_C = 8
ROWS = 256
COLS = 512
N_COL = 2


def draw_bad(key, part):
    key = jax.random.fold_in(key, 11)
    hits = jax.random.randint(key, (ROWS, COLS), 0, 8)
    column = jnp.arange(COLS, dtype=jnp.int32) % 4
    return jnp.where((hits == 0) & (column[None, :] == 1), 1, 0).astype(jnp.int32)


def place_ends(result, rng, smallest, high):
    extent = result.shape
    spot = [jax.random.randint(jax.random.fold_in(rng, axis), (), 0, extent[axis]) for axis in range(len(extent))]
    result = result.at[tuple(spot)].set(smallest)
    longest = extent.index(max(extent))
    spot[longest] = (spot[longest] + 1) % extent[longest]
    return result.at[tuple(spot)].set(high)


def steps_of(stream_key, dims, shards, smallest, high):
    loudness = 1.0
    for axis_at, shards_of in shards:
        steps = jax.random.uniform(jax.random.fold_in(jax.random.fold_in(stream_key, 6), axis_at), (shards_of,), jnp.float32, smallest / len(shards), high / len(shards))
        loudness = loudness * jnp.repeat(jnp.exp(steps), dims[axis_at] // shards_of).reshape((-1,) + (1,) * (len(dims) - 1 - axis_at))
    return loudness


def scatter_about(key, dims, scale, most, kind=jnp.bfloat16):
    values = jax.random.normal(key, dims, jnp.float32) * scale
    return jnp.minimum(jnp.maximum(values, -most), most).astype(kind)


def setup_inputs(seed: int = 0, part: int = 0) -> dict:
    seeds = jax.random.split(jax.random.key(seed), 13)
    own_keys = jax.random.split(jax.random.fold_in(seeds[12], part), 13)
    return {
        "raw": jnp.clip(0.5 + 6.0 * jax.random.uniform(own_keys[0], (FRAMES, ROWS, COLS), jnp.float32) ** steps_of(own_keys[0], (FRAMES, ROWS, COLS), ((0, 4), (1, 2), (2, 2)), -0.2, 0.2), 0.5, 6.5),
        "dark": jnp.clip(0.3 * jax.random.uniform(seeds[1], (ROWS, COLS), jnp.float32) ** steps_of(seeds[1], (ROWS, COLS), ((0, 2), (1, 2)), -0.2, 0.2), 0.0, 0.3),
        "gain": jnp.clip(1.0 + 0.1 * jax.random.normal(seeds[2], (ROWS, COLS), jnp.float32), 0.5, 1.5),
        "bad": draw_bad(jax.random.fold_in(seeds[12], 71), part),
        "taps_col": jnp.clip(jnp.exp(jax.random.uniform(seeds[4], (TAPS,), jnp.float32, math.log(0.015), math.log(0.05))), 0.015, 0.05),
        "taps_row": jnp.clip(jnp.exp(jax.random.uniform(seeds[5], (TAPS,), jnp.float32, math.log(0.015), math.log(0.05))), 0.015, 0.05),
        "levels": place_ends(jax.random.randint(own_keys[6], (FRAMES, GRID_R, GRID_C, MODES), 0, LEVELS), jax.random.fold_in(own_keys[6], 1), 0, LEVELS - 1).astype(jnp.int32),
        "level_table": jnp.clip(jax.random.uniform(seeds[7], (LEVELS,), jnp.float32, -0.6, 0.6), -0.6, 0.6),
        "basis": scatter_about(seeds[8], (MODES, PUPIL * PUPIL), 1.0, 4.0, jnp.float32),
        "apod_index": place_ends(jax.random.randint(seeds[9], (GRID_R, GRID_C), 0, WINDOWS), jax.random.fold_in(seeds[9], 1), 0, WINDOWS - 1).astype(jnp.int32),
        "window_table": jnp.clip(jax.random.uniform(seeds[10], (WINDOWS, PATCH), jnp.float32, 0.2, 1.0), 0.2, 1.0),
        "noise": jnp.clip(jnp.exp(jax.random.uniform(seeds[11], (PATCH, PATCH), jnp.float32, math.log(0.05), math.log(0.5))), 0.05, 0.5),
    }


def dft_tables(length, width):
    freqs = jnp.arange(length, dtype=jnp.int32)[:, None]
    samples = jnp.arange(width, dtype=jnp.int32)[None, :]
    angles = ((freqs * samples) % length).astype(jnp.float32) * (2.0 * math.pi / length)
    return jnp.cos(angles), jnp.sin(angles)


def left_mul(matrix, values):
    return jnp.einsum("kn,...nm->...km", matrix, values, precision=lax.Precision.HIGHEST)


def right_mul(values, matrix):
    return jnp.einsum("...kn,mn->...km", values, matrix, precision=lax.Precision.HIGHEST)


def forward_real(values):
    cosine, sine = dft_tables(values.shape[-1], values.shape[-1])
    cos_rows = left_mul(cosine, values)
    sin_rows = left_mul(sine, values)
    real_part = right_mul(cos_rows, cosine) - right_mul(sin_rows, sine)
    imag_part = -(right_mul(sin_rows, cosine) + right_mul(cos_rows, sine))
    return real_part, imag_part


def forward_pupil(real_in, imag_in, length):
    cosine, sine = dft_tables(length, real_in.shape[-1])
    first_real = left_mul(cosine, real_in) + left_mul(sine, imag_in)
    first_imag = left_mul(cosine, imag_in) - left_mul(sine, real_in)
    real_part = right_mul(first_real, cosine) + right_mul(first_imag, sine)
    imag_part = right_mul(first_imag, cosine) - right_mul(first_real, sine)
    return real_part, imag_part


def inverse_real(real_in, imag_in):
    length = real_in.shape[-1]
    cosine, sine = dft_tables(length, length)
    first_real = left_mul(cosine, real_in) - left_mul(sine, imag_in)
    first_imag = left_mul(cosine, imag_in) + left_mul(sine, real_in)
    return (right_mul(first_real, cosine) - right_mul(first_imag, sine)) / float(length * length)


def aperture(grid):
    offsets = 2 * jnp.arange(grid, dtype=jnp.int32) - (grid - 1)
    radius = offsets[:, None] * offsets[:, None] + offsets[None, :] * offsets[None, :]
    return (radius <= grid * grid).astype(jnp.float32)


def spectra(pixels, level_ids, level_table, basis, stop, length):
    picked = (level_ids[..., None] == jnp.arange(level_table.shape[0], dtype=jnp.int32)).astype(jnp.float32)
    coeffs = jnp.sum(picked * level_table, axis=-1)
    phase = jnp.einsum("...m,mq->...q", coeffs, basis, precision=lax.Precision.HIGHEST)
    grid = stop.shape[0]
    phase = phase.reshape(phase.shape[:-1] + (grid, grid))
    field_real, field_imag = forward_pupil(stop * jnp.cos(phase), stop * jnp.sin(phase), length)
    power = field_real * field_real + field_imag * field_imag
    spread = power / jnp.sum(power, axis=(-2, -1), keepdims=True)
    otf_real, otf_imag = forward_real(spread)
    img_real, img_imag = forward_real(pixels)
    return img_real, img_imag, otf_real, otf_imag


def window_rows(apod_ids, window_table):
    picked = (apod_ids[..., None] == jnp.arange(window_table.shape[0], dtype=jnp.int32)).astype(jnp.float32)
    return jnp.sum(picked[..., None] * window_table, axis=-2)


def cut_patches(padded, row_count, col_count, stride):
    blocks = padded.reshape(row_count + 1, stride, col_count + 1, stride).transpose(2, 0, 1, 3)
    columns = jnp.concatenate([blocks[:-1], blocks[1:]], axis=3)
    return jnp.concatenate([columns[:, :-1], columns[:, 1:]], axis=2)


def restore(num_real, num_imag, power_sum, noise):
    total = power_sum + noise
    estimate = inverse_real(num_real / total, num_imag / total)
    length = noise.shape[0]
    blend = jnp.sin(math.pi * (jnp.arange(length, dtype=jnp.float32) + 0.5) / length) ** 2
    return estimate * blend[:, None] * blend[None, :]


def reference(raw, dark, gain, bad, taps_col, taps_row, levels, level_table, basis, apod_index, window_table, noise):
    stride = PATCH // 2
    half_stride = stride // 2
    half_taps = TAPS // 2
    flat0 = (raw - dark[None]) * gain[None]
    edge = jnp.zeros_like(flat0[:, :, :1])
    before = jnp.concatenate([edge, flat0[:, :, :-1]], axis=2)
    after = jnp.concatenate([flat0[:, :, 1:], edge], axis=2)
    flat = jnp.where(bad[None] == 1, 0.5 * (before + after), flat0)
    widened = jnp.pad(flat, ((0, 0), (0, 0), (half_taps, half_taps)))
    across = jnp.zeros_like(flat)
    for offset in range(TAPS):
        across = across + taps_col[offset] * widened[:, :, offset:offset + COLS]
    widened = jnp.pad(across, ((0, 0), (half_taps, half_taps), (0, 0)))
    stray = jnp.zeros_like(flat)
    for offset in range(TAPS):
        stray = stray + taps_row[offset] * widened[:, offset:offset + ROWS, :]
    corrected = flat - stray
    padded = jnp.pad(corrected, ((0, 0), (half_stride, half_stride), (half_stride, half_stride)))
    windows = window_rows(apod_index.T, window_table)
    weights = windows[..., :, None] * windows[..., None, :]
    stop = aperture(PUPIL)

    def frame_step(carry, inputs):
        frame_image, frame_ids = inputs
        pixels = cut_patches(frame_image, GRID_R, GRID_C, stride) * weights
        img_real, img_imag, otf_real, otf_imag = spectra(pixels, frame_ids.transpose(1, 0, 2), level_table, basis, stop, PATCH)
        return (carry[0] + otf_real * img_real + otf_imag * img_imag,
                carry[1] + otf_real * img_imag - otf_imag * img_real,
                carry[2] + otf_real * otf_real + otf_imag * otf_imag), None

    zeros = jnp.zeros((GRID_C, GRID_R, PATCH, PATCH), jnp.float32)
    sums, unused = lax.scan(frame_step, (zeros, zeros, zeros), (padded, levels))
    contrib = restore(sums[0], sums[1], sums[2], noise)
    quads = contrib.reshape(GRID_C, GRID_R, 2, stride, 2, stride).transpose(1, 0, 2, 4, 3, 5)
    nopad = (0, 0)
    grid = (jnp.pad(quads[:, :, 0, 0], ((0, 1), (0, 1), nopad, nopad))
            + jnp.pad(quads[:, :, 0, 1], ((0, 1), (1, 0), nopad, nopad))
            + jnp.pad(quads[:, :, 1, 0], ((1, 0), (0, 1), nopad, nopad))
            + jnp.pad(quads[:, :, 1, 1], ((1, 0), (1, 0), nopad, nopad)))
    assembled = grid.transpose(0, 2, 1, 3).reshape((GRID_R + 1) * stride, (GRID_C + 1) * stride)
    assembled = assembled[half_stride:half_stride + ROWS, half_stride:half_stride + COLS]
    return assembled.reshape(ROWS, N_COL, COLS // N_COL)
```

```python
import math

import jax
import jax.numpy as jnp
from jax import lax
from jax.sharding import PartitionSpec as P

PATCH = 128
PUPIL = 64
TAPS = 31
STEP = 64


def with_halo(value, sides, width, wrap):
    for axis, dim in sides:
        size, length = (lax.axis_size(axis), value.shape[dim])
        up = [(i, (i + 1) % size) for i in range(size if wrap else size - 1)]
        down = [(j, i) for i, j in up]
        last = lax.slice_in_dim(value, length - width, length, axis=dim)
        leading = lax.slice_in_dim(value, 0, width, axis=dim)
        before = lax.ppermute(last, axis, up)
        after = lax.ppermute(leading, axis, down)
        value = jnp.concatenate([before, value, after], axis=dim)
    return value


def dft_tables(length, width):
    freqs = jnp.arange(length, dtype=jnp.int32)[:, None]
    samples = jnp.arange(width, dtype=jnp.int32)[None, :]
    angles = (freqs * samples % length).astype(jnp.float32) * (2.0 * math.pi / length)
    return (jnp.cos(angles), jnp.sin(angles))


def left_mul(matrix, values):
    return jnp.einsum("kn,...nm->...km", matrix, values, precision=lax.Precision.HIGH)


def right_mul(values, matrix):
    return jnp.einsum("...kn,mn->...km", values, matrix, precision=lax.Precision.HIGH)


def forward_real(values):
    cosine, sine = dft_tables(values.shape[-1], values.shape[-1])
    cos_rows = left_mul(cosine, values)
    sin_rows = left_mul(sine, values)
    real_part = right_mul(cos_rows, cosine) - right_mul(sin_rows, sine)
    imag_part = -(right_mul(sin_rows, cosine) + right_mul(cos_rows, sine))
    return (real_part, imag_part)


def forward_pupil(real_in, imag_in, length):
    cosine, sine = dft_tables(length, real_in.shape[-1])
    first_real = left_mul(cosine, real_in) + left_mul(sine, imag_in)
    first_imag = left_mul(cosine, imag_in) - left_mul(sine, real_in)
    real_part = right_mul(first_real, cosine) + right_mul(first_imag, sine)
    imag_part = right_mul(first_imag, cosine) - right_mul(first_real, sine)
    return (real_part, imag_part)


def inverse_real(real_in, imag_in):
    length = real_in.shape[-1]
    cosine, sine = dft_tables(length, length)
    first_real = left_mul(cosine, real_in) - left_mul(sine, imag_in)
    first_imag = left_mul(cosine, imag_in) + left_mul(sine, real_in)
    return (right_mul(first_real, cosine) - right_mul(first_imag, sine)) / float(length * length)


def aperture(grid):
    offsets = 2 * jnp.arange(grid, dtype=jnp.int32) - (grid - 1)
    radius = offsets[:, None] * offsets[:, None] + offsets[None, :] * offsets[None, :]
    return (radius <= grid * grid).astype(jnp.float32)


def spectra(pixels, coeffs, basis, stop, length):
    phase = jnp.einsum("...m,mq->...q", coeffs, basis, precision=lax.Precision.HIGHEST)
    grid = stop.shape[0]
    phase = phase.reshape(phase.shape[:-1] + (grid, grid))
    field_real, field_imag = forward_pupil(stop * jnp.cos(phase), stop * jnp.sin(phase), length)
    power = field_real * field_real + field_imag * field_imag
    spread = power / jnp.sum(power, axis=(-2, -1), keepdims=True)
    otf_real, otf_imag = forward_real(spread)
    img_real, img_imag = forward_real(pixels)
    return (img_real, img_imag, otf_real, otf_imag)


def window_rows(apod_ids, window_table):
    picked = (apod_ids[..., None] == jnp.arange(window_table.shape[0], dtype=jnp.int32)).astype(
        jnp.float32
    )
    return jnp.sum(picked[..., None] * window_table, axis=-2)


def cut_patches(padded, row_count, col_count, stride):
    blocks = padded.reshape(row_count + 1, stride, col_count + 1, stride).transpose(2, 0, 1, 3)
    columns = jnp.concatenate([blocks[:-1], blocks[1:]], axis=3)
    return jnp.concatenate([columns[:, :-1], columns[:, 1:]], axis=2)


def restore(num_real, num_imag, power_sum, noise):
    total = power_sum + noise
    estimate = inverse_real(num_real / total, num_imag / total)
    length = noise.shape[0]
    blend = jnp.sin(math.pi * (jnp.arange(length, dtype=jnp.float32) + 0.5) / length) ** 2
    return estimate * blend[:, None] * blend[None, :]


def frame_products(img_real, img_imag, otf_real, otf_imag):
    return (
        otf_real * img_real + otf_imag * img_imag,
        otf_real * img_imag - otf_imag * img_real,
        otf_real * otf_real + otf_imag * otf_imag,
    )


def band(taps, count, width):
    lag = jnp.arange(width, dtype=jnp.int32)[None, :] - jnp.arange(count, dtype=jnp.int32)[:, None]
    matrix = jnp.zeros((count, width), jnp.float32)
    for offset in range(taps.shape[0]):
        matrix = jnp.where(lag == offset, taps[offset], matrix)
    return matrix


def stray_light(widened, taps_col, taps_row, out_rows, out_cols):
    across = right_mul(widened, band(taps_col, out_cols, widened.shape[1]))
    return left_mul(band(taps_row, out_rows, widened.shape[0]), across)


def per_device(
    raw,
    dark,
    gain,
    bad,
    taps_col,
    taps_row,
    levels,
    level_table,
    basis,
    apod_index,
    window_table,
    noise,
):
    tile_rows, tile_cols = dark.shape
    stride = STEP
    half_stride = STEP // 2
    half_taps = TAPS // 2
    patch_rows, patch_cols = apod_index.shape
    flat0 = (raw[0] - dark) * gain
    edge = jnp.zeros_like(flat0[:, :1])
    before = jnp.concatenate([edge, flat0[:, :-1]], axis=1)
    after = jnp.concatenate([flat0[:, 1:], edge], axis=1)
    flat = jnp.where(bad == 1, 0.5 * (before + after), flat0)
    widened = with_halo(flat, (("row", 0), ("col", 1)), half_taps, False)
    corrected = flat - stray_light(widened, taps_col, taps_row, tile_rows, tile_cols)
    padded = with_halo(corrected, (("row", 0), ("col", 1)), half_stride, False)
    windows = window_rows(apod_index.T, window_table)
    weights = windows[..., :, None] * windows[..., None, :]
    level_ids = levels[0].transpose(1, 0, 2)
    picked = (level_ids[..., None] == jnp.arange(level_table.shape[0], dtype=jnp.int32)).astype(
        jnp.float32
    )
    coeffs = jnp.sum(picked * level_table, axis=-1)
    modes = coeffs.shape[-1]
    block = jnp.pad(coeffs, ((0, 0), (0, -patch_rows % 8), (0, PATCH - modes)))
    strips = jnp.stack(
        [padded[:, b * stride : b * stride + PATCH] for b in range(patch_cols)], axis=0
    )
    packed = jnp.concatenate([strips, block], axis=1)
    received = lax.all_to_all(packed, "frame", split_axis=0, concat_axis=0, tiled=True)
    height = strips.shape[1]
    coeffs = received[:, height : height + patch_rows, :modes]
    patches = jnp.stack(
        [received[:, a * stride : a * stride + PATCH] for a in range(patch_rows)], axis=1
    )
    own = lax.dynamic_index_in_dim(weights, lax.axis_index("frame"), 0, keepdims=False)
    img_real, img_imag, otf_real, otf_imag = spectra(
        patches * own, coeffs, basis, aperture(PUPIL), PATCH
    )
    num_real, num_imag, power_sum = frame_products(img_real, img_imag, otf_real, otf_imag)
    contrib = restore(
        jnp.sum(num_real, axis=0), jnp.sum(num_imag, axis=0), jnp.sum(power_sum, axis=0), noise
    )
    sideways = with_halo(contrib, (("frame", 2),), half_stride, True)
    left_rim = sideways[:, :, :half_stride]
    right_rim = sideways[:, :, sideways.shape[2] - half_stride :]
    paired = jnp.stack([right_rim, left_rim], axis=0)
    beyond = with_halo(paired, (("col", 0),), 1, False)
    strip = lax.axis_index("frame")
    left_part = jnp.where(strip == 0, beyond[0], left_rim)
    right_part = jnp.where(strip == lax.axis_size("frame") - 1, beyond[3], right_rim)
    columns = contrib[:, :, half_stride : half_stride + stride] + jnp.concatenate(
        [left_part, right_part], axis=2
    )
    upper = columns[:, :stride]
    lower = columns[:, stride:]
    blank = jnp.zeros((1, stride, stride), jnp.float32)
    stacked = jnp.concatenate([upper, blank], axis=0) + jnp.concatenate([blank, lower], axis=0)
    stacked = stacked.reshape((patch_rows + 1) * stride, stride)
    vertical = with_halo(stacked, (("row", 0),), half_stride, False)
    mine = vertical[stride : stride + tile_rows]
    above = vertical[:half_stride]
    below = vertical[vertical.shape[0] - half_stride :]
    middle = jnp.zeros((tile_rows - stride, stride), jnp.float32)
    restored = mine + jnp.concatenate([above, middle, below], axis=0)
    return restored[:, None, :]


def solution(mesh):
    placed = (
        P(("groups", "frame"), "row", "col"),
        P("row", "col"),
        P("row", "col"),
        P("row", "col"),
        P(),
        P(),
        P(("groups", "frame"), "row", "col", None),
        P(),
        P(),
        P("row", "col"),
        P(),
        P(),
    )
    return jax.shard_map(
        per_device,
        mesh=mesh,
        in_specs=placed,
        out_specs=P(("groups", "row"), "col", "frame"),
        check_vma=False,
    )
```

```python
import functools
import math

import jax
import jax.numpy as jnp
import ml_dtypes
import numpy as np
from jax import lax
from jax.experimental import pallas as pl
from jax.experimental.pallas import tpu as pltpu
from jax.sharding import PartitionSpec as P

PATCH = 128
PUPIL = 64
STEP = 64
HALF = 32
RIM = 48
KEPT = 72
MESH = pl.DeviceIdType.MESH
AROUND = [(i, j) for i in (-1, 0, 1) for j in (-1, 0, 1) if (i, j) != (0, 0)]


def split_table(table):
    table = table.astype(np.float32)
    high = table.astype(ml_dtypes.bfloat16)
    return high, (table - high.astype(np.float32)).astype(ml_dtypes.bfloat16)


def tables():
    n = PATCH
    turn = np.outer(np.arange(n), np.arange(n)) % n * (2.0 * math.pi / n)
    cosine, sine = np.cos(turn), np.sin(turn)
    blend = np.sin(math.pi * (np.arange(n) + 0.5) / n) ** 2
    pupil_x = np.zeros((2, 2, PUPIL, 2, 2, n))
    for q in range(2):
        pupil_x[0, q, :, q, 0] = cosine[:PUPIL]
        pupil_x[0, q, :, q, 1] = -sine[:PUPIL]
        pupil_x[1, q, :, q, 0] = sine[:PUPIL]
        pupil_x[1, q, :, q, 1] = cosine[:PUPIL]
    order = np.array([2 * j + q for q in range(2) for j in range(PUPIL // 2)])
    c, s = cosine[:, order], sine[:, order]
    pupil_y = np.block([[c, s], [-s, c]])
    half = n // 2 + 1
    front = np.zeros((2 * KEPT, n))
    front[:half] = cosine[:half]
    front[KEPT : KEPT + half] = sine[:half]
    across = np.block([[cosine, -sine], [-sine, -cosine]])
    back_x = np.block([[cosine, sine], [-sine, cosine]]) * np.tile(blend, 2)[None, :]
    weight = np.where((np.arange(half) % (n // 2)) == 0, 1.0, 2.0) / (n * n)
    back_y = np.zeros((n, 2 * KEPT))
    back_y[:, :half] = cosine[:, :half] * weight * blend[:, None]
    back_y[:, KEPT : KEPT + half] = -sine[:, :half] * weight * blend[:, None]
    found = []
    for table in (pupil_x.reshape(256, 512), pupil_y, front, across, back_x, back_y):
        found.extend(split_table(table))
    return found


def halves(value):
    high = value.astype(jnp.bfloat16)
    return high, (value - high.astype(jnp.float32)).astype(jnp.bfloat16)


def dot(left, right):
    return jnp.dot(left, right, preferred_element_type=jnp.float32)


def dot3(left, right):
    return dot(left[0], right[0]) + (dot(left[1], right[0]) + dot(left[0], right[1]))


def cos_sin(angle):
    quarter = jnp.floor(angle * (2.0 / math.pi) + 0.5)
    rest = (angle - quarter * 1.5703125) - quarter * (math.pi / 2 - 1.5703125)
    sq = rest * rest
    s = rest + rest * sq * (-1 / 6 + sq * (1 / 120 + sq * (-1 / 5040 + sq * (1 / 362880))))
    c = 1.0 + sq * (-0.5 + sq * (1 / 24 + sq * (-1 / 720 + sq * (1 / 40320))))
    turn = quarter.astype(jnp.int32) & 3
    odd = (turn & 1) == 1
    cos_value, sin_value = jnp.where(odd, s, c), jnp.where(odd, c, s)
    return (
        jnp.where((turn == 1) | (turn == 2), -cos_value, cos_value),
        jnp.where(turn >= 2, -sin_value, sin_value),
    )


def band(taps, shape, lag):
    matrix = jnp.zeros(shape, jnp.float32)
    for t in range(taps.shape[0]):
        matrix = jnp.where(lag == t, taps[t], matrix)
    return halves(matrix)


def kernel(
    sizes,
    raw, dark, gain, bad, taps_col, taps_row, levels, level_table, basis, apod, window_table, noise,
    px_h, px_l, py_h, py_l, fr_h, fr_l, ac_h, ac_l, bx_h, bx_l, by_h, by_l,
    out,
    ext, coeff, coeff_all, phase_s, stage, strips, strip_s, pack, rims,
    a_send, a_recv, q_send, q_recv, b_send, b_recv, c_send, c_recv,
):
    frames, rows, cols = sizes
    g, me = lax.axis_index("groups"), lax.axis_index("frame")
    r, c = lax.axis_index("row"), lax.axis_index("col")
    tile_rows, tile_cols = dark.shape
    h = c * frames + me

    def inside(i, size):
        return (i >= 0) & (i < size)

    def tile_ok(dr, dc):
        return inside(r + dr, rows) & inside(c + dc, cols)

    def strip_ok(dr, dh):
        return inside(r + dr, rows) & inside(h + dh, cols * frames)

    def strip_device(dr, dh):
        to = h + dh
        return (g, to % frames, r + dr, to // frames)

    def peer(step):
        return (me + step) % frames

    barrier = pltpu.get_barrier_semaphore()
    expected = jnp.int32(frames - 1)
    for step in range(1, frames):
        pl.semaphore_signal(barrier, inc=1, device_id=(g, peer(step), r, c), device_id_type=MESH)
    for dr, dc in AROUND:
        ok = tile_ok(dr, dc)
        expected = expected + ok.astype(jnp.int32)

        @pl.when(ok)
        def _(dr=dr, dc=dc):
            pl.semaphore_signal(
                barrier, inc=1, device_id=(g, me, r + dr, c + dc), device_id_type=MESH
            )

        if dc:
            ok = strip_ok(dr, dc)
            expected = expected + ok.astype(jnp.int32)

            @pl.when(ok)
            def _(dr=dr, dc=dc):
                pl.semaphore_signal(
                    barrier, inc=1, device_id=strip_device(dr, dc), device_id_type=MESH
                )

    flat0 = (raw[0] - dark[...]) * gain[...]
    mean = 0.5 * (pltpu.roll(flat0, 1, 1) + pltpu.roll(flat0, tile_cols - 1, 1))
    ext[RIM : RIM + tile_rows, PATCH : PATCH + tile_cols] = jnp.where(bad[...] == 1, mean, flat0)
    ids = levels[...]
    picked = jnp.zeros(ids.shape, jnp.float32)
    for v in range(level_table.shape[0]):
        picked = jnp.where(ids == v, level_table[v], picked)
    modes = ids.shape[1]
    coeff[...] = jnp.zeros(coeff.shape, jnp.float32)
    coeff[:, :modes] = picked
    coeff_all[me] = coeff[...]

    row_src = {0: pl.ds(RIM, tile_rows), 1: pl.ds(tile_rows, RIM), -1: pl.ds(RIM, RIM)}
    row_dst = {0: pl.ds(RIM, tile_rows), 1: pl.ds(0, RIM), -1: pl.ds(RIM + tile_rows, RIM)}
    col_src = {0: pl.ds(PATCH, tile_cols), 1: pl.ds(tile_cols, PATCH), -1: pl.ds(PATCH, PATCH)}
    col_dst = {0: pl.ds(PATCH, tile_cols), 1: pl.ds(0, PATCH), -1: pl.ds(PATCH + tile_cols, PATCH)}

    def a_copy(i):
        dr, dc = AROUND[i]
        return pltpu.make_async_remote_copy(
            src_ref=ext.at[row_src[dr], col_src[dc]],
            dst_ref=ext.at[row_dst[dr], col_dst[dc]],
            send_sem=a_send.at[i],
            recv_sem=a_recv.at[i],
            device_id=(g, me, r + dr, c + dc),
            device_id_type=MESH,
        )

    def q_copy(step, source):
        return pltpu.make_async_remote_copy(
            src_ref=coeff,
            dst_ref=coeff_all.at[source],
            send_sem=q_send.at[step],
            recv_sem=q_recv.at[source],
            device_id=(g, peer(step), r, c),
            device_id_type=MESH,
        )

    height = strips.shape[1]
    if rows == 2:
        sent = pl.ds(pl.multiple_of(HALF * (1 - r), HALF), height - HALF)
    else:
        sent = pl.ds(0, height)

    def b_copy(k, source):
        return pltpu.make_async_remote_copy(
            src_ref=stage.at[k, sent],
            dst_ref=strips.at[source, sent],
            send_sem=b_send.at[k],
            recv_sem=b_recv.at[source],
            device_id=(g, k, r, c),
            device_id_type=MESH,
        )

    def c_copy(i):
        dr, dh = AROUND[i]
        source = {
            0: pack.at[(dh + 1) // 2],
            -1: strip_s.at[pl.ds(0, HALF)],
            1: strip_s.at[pl.ds(height - HALF, HALF)],
        }[dr]
        return pltpu.make_async_remote_copy(
            src_ref=source,
            dst_ref=rims.at[i],
            send_sem=c_send.at[i],
            recv_sem=c_recv.at[i],
            device_id=strip_device(dr, dh),
            device_id_type=MESH,
        )

    pl.semaphore_wait(barrier, expected)
    for i, (dr, dc) in enumerate(AROUND):

        @pl.when(tile_ok(dr, dc))
        def _(i=i):
            a_copy(i).start()

    for step in range(1, frames):
        q_copy(step, me).start()

    for i, (dr, dc) in enumerate(AROUND):

        @pl.when(jnp.logical_not(tile_ok(-dr, -dc)))
        def _(dr=dr, dc=dc):
            y, x = row_dst[dr], col_dst[dc]
            ext[y, x] = jnp.zeros((y.size, x.size), jnp.float32)

        @pl.when(jnp.logical_not(strip_ok(-dr, -dc)))
        def _(i=i):
            rims[i] = jnp.zeros(rims.shape[1:], jnp.float32)

    lag = lax.broadcasted_iota(jnp.int32, (256, PATCH), 0) - lax.broadcasted_iota(
        jnp.int32, (256, PATCH), 1
    )
    col_bands = [band(taps_col, lag.shape, lag - first) for first in (81, 17)]
    shape = (height, ext.shape[0])
    lag = lax.broadcasted_iota(jnp.int32, shape, 1) - lax.broadcasted_iota(jnp.int32, shape, 0)
    row_band = band(taps_row, shape, lag - 1)
    y_at = lax.broadcasted_iota(jnp.int32, (PATCH, PATCH), 0)
    x_at = lax.broadcasted_iota(jnp.int32, (PATCH, PATCH), 1)
    flip = ((y_at + x_at) % PATCH == 0).astype(jnp.float32).astype(jnp.bfloat16)
    n_high, n_low = halves(noise[...])
    turned = dot(flip, n_high), dot(flip, n_low)
    turned = dot(turned[0].astype(jnp.bfloat16), flip) + dot(turned[1].astype(jnp.bfloat16), flip)
    noises = (noise[:KEPT, :], turned[:KEPT, :])
    weights = []
    for a in range(2):
        chosen = apod[a, me]
        line = jnp.zeros((1, PATCH), jnp.float32)
        for v in range(window_table.shape[0]):
            line = jnp.where(chosen == v, window_table[v : v + 1, :], line)
        column = jnp.sum(jnp.where(y_at == x_at, line, 0.0), axis=1, keepdims=True)
        weights.append(column * line)
    basis_parts = halves(basis[...])

    for i, (dr, dc) in enumerate(AROUND):

        @pl.when(tile_ok(-dr, -dc))
        def _(i=i):
            a_copy(i).wait_recv()

    shape = (height, PATCH)
    y_all = lax.broadcasted_iota(jnp.int32, shape, 0) + (r * tile_rows - HALF)
    x_all = lax.broadcasted_iota(jnp.int32, shape, 1) + (c * tile_cols - HALF)
    for k in range(frames):
        first = (STEP * k + 81) // PATCH * PATCH
        block = ext[:, first : first + 256]
        light = dot3(halves(block), col_bands[k % 2])
        stray = dot3(row_band, halves(light))
        at = STEP * k + 96 - first
        here = pltpu.roll(block[16 : 16 + height], 256 - at, 1)[:, :PATCH]
        x_here = x_all + STEP * k
        keep = inside(y_all, rows * tile_rows) & inside(x_here, cols * tile_cols)
        stage[k] = jnp.where(keep, here - stray, 0.0)

        @pl.when(k != me)
        def _(k=k):
            b_copy(k, me).start()

    strips[me] = stage[me]
    if rows == 2:
        edge = pl.ds(pl.multiple_of((height - HALF) * r, HALF), HALF)
        for step in range(1, frames):
            strips[peer(step), edge, :] = jnp.zeros((HALF, PATCH), jnp.float32)

    for step in range(1, frames):
        q_copy(step, peer(step)).wait_recv()
    count = 2 * frames
    mine = [
        coeff_all[peer(step), pl.ds(a * frames + me, 1), :]
        for step in range(frames)
        for a in range(2)
    ]
    phase = dot3(halves(jnp.concatenate(mine, axis=0)[:, :modes]), basis_parts)
    lines = PUPIL // 2
    for j in range(lines):
        phase_s[pl.ds(j, count, stride=lines), :] = phase[:, j * PATCH : (j + 1) * PATCH]
    y2 = 2 * (2 * y_at[:lines] + x_at[:lines] // PUPIL) - (PUPIL - 1)
    x2 = 2 * (x_at[:lines] % PUPIL) - (PUPIL - 1)
    stop = (y2 * y2 + x2 * x2 <= PUPIL * PUPIL).astype(jnp.float32)
    stop = jnp.concatenate([stop] * count, axis=0)
    real, imag = cos_sin(phase_s[...])
    field = jnp.concatenate([real * stop, imag * stop], axis=1)
    field = dot3(halves(field), (px_h[...], px_l[...]))
    picks = []
    for p in range(count):
        part = field[p * lines : (p + 1) * lines]
        picks.append(
            jnp.concatenate([part[:, q * PATCH : (q + 1) * PATCH] for q in (0, 2, 1, 3)], axis=0)
        )

    def spectrum(images):
        first = dot3((fr_h[...], fr_l[...]), halves(jnp.concatenate(images, axis=1)))
        parts = [
            jnp.concatenate(
                [
                    first[:KEPT, i * PATCH : (i + 1) * PATCH],
                    first[KEPT:, i * PATCH : (i + 1) * PATCH],
                ],
                axis=1,
            )
            for i in range(len(images))
        ]
        return dot3(halves(jnp.concatenate(parts, axis=0)), (ac_h[...], ac_l[...]))

    optics = []
    for step in range(frames):
        pair = jnp.concatenate(picks[2 * step : 2 * step + 2], axis=1)
        spread = dot3((py_h[...], py_l[...]), halves(pair))
        power = spread[:PATCH] * spread[:PATCH] + spread[PATCH:] * spread[PATCH:]
        images = []
        for a in range(2):
            one = power[:, a * PATCH : (a + 1) * PATCH]
            images.append(one * (1.0 / jnp.sum(one, axis=(0, 1), keepdims=True)))
        optics.append(spectrum(images))

    totals = [[jnp.zeros((KEPT, PATCH), jnp.float32)] * 3 for a in range(2)]
    for step in range(frames):
        if step:
            b_copy(peer(step), peer(step)).wait_recv()
        images = [
            strips[peer(step), a * STEP : a * STEP + PATCH, :] * weights[a] for a in range(2)
        ]
        image = spectrum(images)
        for a in range(2):
            lot = slice(a * KEPT, (a + 1) * KEPT)
            i_re, i_im = image[lot, :PATCH], image[lot, PATCH:]
            o_re, o_im = optics[step][lot, :PATCH], optics[step][lot, PATCH:]
            total = totals[a]
            totals[a] = [
                total[0] + o_re * i_re + o_im * i_im,
                total[1] + o_re * i_im - o_im * i_re,
                total[2] + o_re * o_re + o_im * o_im,
            ]

    whole = []
    for a in range(2):
        num_re, num_im, power = totals[a]
        factor = 0.5 / (power + noises[0]) + 0.5 / (power + noises[1])
        whole.append(jnp.concatenate([num_re * factor, num_im * factor], axis=1))
    turned = dot3(halves(jnp.concatenate(whole, axis=0)), (bx_h[...], bx_l[...]))
    sides = [
        jnp.concatenate(
            [turned[a * KEPT : (a + 1) * KEPT, :PATCH], turned[a * KEPT : (a + 1) * KEPT, PATCH:]],
            axis=0,
        )
        for a in range(2)
    ]
    contrib = dot3((by_h[...], by_l[...]), halves(jnp.concatenate(sides, axis=1)))
    upper, lower = contrib[:, :PATCH], contrib[:, PATCH:]
    strip = jnp.concatenate([upper[:STEP], upper[STEP:] + lower[:STEP], lower[STEP:]], axis=0)
    strip_s[...] = strip
    body = strip[HALF : HALF + tile_rows]
    lane = lax.broadcasted_iota(jnp.int32, (HALF, PATCH), 1)
    for side in range(2):
        packed = jnp.zeros((HALF, PATCH), jnp.float32)
        for q in range(4):
            shift = (HALF * q + HALF * side) % PATCH
            rolled = body[q * HALF : (q + 1) * HALF]
            if shift:
                rolled = pltpu.roll(rolled, shift, 1)
            packed = jnp.where(lane // HALF == q, rolled, packed)
        pack[side] = packed
    for i, (dr, dh) in enumerate(AROUND):

        @pl.when(strip_ok(dr, dh))
        def _(i=i):
            c_copy(i).start()

    for i, (dr, dc) in enumerate(AROUND):

        @pl.when(tile_ok(dr, dc))
        def _(i=i):
            a_copy(i).wait_send()

    for step in range(1, frames):
        q_copy(step, me).wait_send()
        b_copy(peer(step), me).wait_send()

    for i, (dr, dh) in enumerate(AROUND):

        @pl.when(strip_ok(-dr, -dh))
        def _(i=i):
            c_copy(i).wait_recv()

    from_left, from_right = lane // HALF == 1, lane // HALF == 2
    blocks = []
    for q in range(4):
        value = body[q * HALF : (q + 1) * HALF]
        for i, (dr, dh) in enumerate(AROUND):
            if dr == 0:
                goal = 1 if dh == 1 else 2
                shift = (HALF * (goal - q)) % PATCH
                got = pltpu.roll(rims[i], shift, 1) if shift else rims[i]
                value = value + jnp.where(from_left if dh == 1 else from_right, got, 0.0)
            elif (dr == 1 and q == 0) or (dr == -1 and q == 3):
                if dh == 0:
                    value = value + rims[i]
                else:
                    got = pltpu.roll(rims[i], STEP, 1)
                    value = value + jnp.where(from_left if dh == 1 else from_right, got, 0.0)
        blocks.append(pltpu.roll(value, PATCH - HALF, 1)[:, :STEP])
    out[...] = jnp.concatenate(blocks, axis=0)

    for i, (dr, dh) in enumerate(AROUND):

        @pl.when(strip_ok(dr, dh))
        def _(i=i):
            c_copy(i).wait_send()


def per_device(
    sizes,
    raw, dark, gain, bad, taps_col, taps_row, levels, level_table, basis, apod_index, window_table, noise,
):
    frames = sizes[0]
    tile_rows, tile_cols = dark.shape
    height = tile_rows + STEP
    count = 2 * frames
    vmem = pl.BlockSpec(memory_space=pltpu.VMEM)
    smem = pl.BlockSpec(memory_space=pltpu.SMEM)
    in_specs = [vmem] * 4 + [smem, smem, vmem, smem, vmem, smem, vmem, vmem] + [vmem] * 12
    dma = pltpu.SemaphoreType.DMA
    restored = pl.pallas_call(
        functools.partial(kernel, sizes),
        out_shape=jax.ShapeDtypeStruct((tile_rows, STEP), jnp.float32),
        in_specs=in_specs,
        out_specs=vmem,
        scratch_shapes=[
            pltpu.VMEM((tile_rows + 2 * RIM, tile_cols + 2 * PATCH), jnp.float32),
            pltpu.VMEM((count, PATCH), jnp.float32),
            pltpu.VMEM((frames, count, PATCH), jnp.float32),
            pltpu.VMEM((count * PUPIL // 2, PATCH), jnp.float32),
            pltpu.VMEM((frames, height, PATCH), jnp.float32),
            pltpu.VMEM((frames, height, PATCH), jnp.float32),
            pltpu.VMEM((height, PATCH), jnp.float32),
            pltpu.VMEM((2, HALF, PATCH), jnp.float32),
            pltpu.VMEM((8, HALF, PATCH), jnp.float32),
            dma((8,)),
            dma((8,)),
            dma((frames,)),
            dma((frames,)),
            dma((frames,)),
            dma((frames,)),
            dma((8,)),
            dma((8,)),
        ],
        compiler_params=pltpu.CompilerParams(
            collective_id=0, has_side_effects=True, vmem_limit_bytes=48 * 1024 * 1024
        ),
    )(
        raw, dark, gain, bad, taps_col, taps_row,
        levels.reshape(count, levels.shape[3]),
        level_table, basis, apod_index, window_table, noise,
        *[jnp.asarray(table) for table in tables()],
    )
    return restored[:, None, :]


def solution(mesh):
    placed = (
        P(("groups", "frame"), "row", "col"),
        P("row", "col"),
        P("row", "col"),
        P("row", "col"),
        P(),
        P(),
        P(("groups", "frame"), "row", "col", None),
        P(),
        P(),
        P("row", "col"),
        P(),
        P(),
    )
    sizes = (mesh.shape["frame"], mesh.shape["row"], mesh.shape["col"])
    return jax.shard_map(
        functools.partial(per_device, sizes),
        mesh=mesh,
        in_specs=placed,
        out_specs=P(("groups", "row"), "col", "frame"),
        check_vma=False,
    )
```

```python
import functools
import math

import jax
import jax.numpy as jnp
import ml_dtypes
import numpy as np
from jax import lax
from jax.experimental import pallas as pl
from jax.experimental.pallas import tpu as pltpu
from jax.sharding import PartitionSpec as P

PATCH = 128
PUPIL = 64
STEP = 64
HALF = 32
RIM = 48
KEPT = 72
MESH = pl.DeviceIdType.MESH
AROUND = [(i, j) for i in (-1, 0, 1) for j in (-1, 0, 1) if (i, j) != (0, 0)]


def split_table(table):
    table = table.astype(np.float32)
    high = table.astype(ml_dtypes.bfloat16)
    return high, (table - high.astype(np.float32)).astype(ml_dtypes.bfloat16)


def tables():
    n = PATCH
    turn = np.outer(np.arange(n), np.arange(n)) % n * (2.0 * math.pi / n)
    cosine, sine = np.cos(turn), np.sin(turn)
    blend = np.sin(math.pi * (np.arange(n) + 0.5) / n) ** 2
    pupil_x = np.zeros((2, 2, PUPIL, 2, 2, n))
    for q in range(2):
        pupil_x[0, q, :, q, 0] = cosine[:PUPIL]
        pupil_x[0, q, :, q, 1] = -sine[:PUPIL]
        pupil_x[1, q, :, q, 0] = sine[:PUPIL]
        pupil_x[1, q, :, q, 1] = cosine[:PUPIL]
    order = np.array([2 * j + q for q in range(2) for j in range(PUPIL // 2)])
    c, s = cosine[:, order], sine[:, order]
    pupil_y = np.block([[c, s], [-s, c]])
    half = n // 2 + 1
    front = np.zeros((2 * KEPT, n))
    front[:half] = cosine[:half]
    front[KEPT : KEPT + half] = sine[:half]
    across = np.block([[cosine, -sine], [-sine, -cosine]])
    back_x = np.block([[cosine, sine], [-sine, cosine]]) * np.tile(blend, 2)[None, :]
    weight = np.where((np.arange(half) % (n // 2)) == 0, 1.0, 2.0) / (n * n)
    back_y = np.zeros((n, 2 * KEPT))
    back_y[:, :half] = cosine[:, :half] * weight * blend[:, None]
    back_y[:, KEPT : KEPT + half] = -sine[:, :half] * weight * blend[:, None]
    pupil_x = pupil_x.reshape(256, 2, 256)
    side = np.zeros((256, 256))
    side[:, :n] = pupil_y
    side[: 2 * KEPT, n:] = front
    last = np.zeros((n, 256))
    last[:, : 2 * KEPT] = back_y
    whole = [pupil_x[:, 0], pupil_x[:, 1], across, back_x, side, last]
    return np.stack(split_table(np.concatenate(whole, axis=0)))


def halves(value):
    high = value.astype(jnp.bfloat16)
    return high, (value - high.astype(jnp.float32)).astype(jnp.bfloat16)


def dot(left, right):
    return jnp.dot(left, right, preferred_element_type=jnp.float32)


def dot3(left, right):
    return dot(left[0], right[0]) + (dot(left[1], right[0]) + dot(left[0], right[1]))


def cos_sin(angle):
    quarter = jnp.floor(angle * (2.0 / math.pi) + 0.5)
    rest = (angle - quarter * 1.5703125) - quarter * (math.pi / 2 - 1.5703125)
    sq = rest * rest
    s = rest + rest * sq * (-1 / 6 + sq * (1 / 120 + sq * (-1 / 5040 + sq * (1 / 362880))))
    c = 1.0 + sq * (-0.5 + sq * (1 / 24 + sq * (-1 / 720 + sq * (1 / 40320))))
    turn = quarter.astype(jnp.int32) & 3
    odd = (turn & 1) == 1
    cos_value, sin_value = jnp.where(odd, s, c), jnp.where(odd, c, s)
    return (
        jnp.where((turn == 1) | (turn == 2), -cos_value, cos_value),
        jnp.where(turn >= 2, -sin_value, sin_value),
    )


def band(taps, shape, lag):
    matrix = jnp.zeros(shape, jnp.float32)
    for t in range(taps.shape[0]):
        matrix = jnp.where(lag == t, taps[t], matrix)
    return halves(matrix)


def kernel(
    sizes,
    *refs,
):
    given, refs = refs[:13], refs[13:]
    out, held, refs = refs[0], refs[1:14], refs[14:]
    (raw, dark, gain, bad, taps_col, taps_row, levels, level_table, basis, apod, window_table, noise,
     table) = held
    (ext, coeff, coeff_all, phase_s, stage, strips, strip_s, pack, rims,
     a_send, a_recv, q_send, q_recv, b_send, b_recv, c_send, c_recv, in_sem) = refs
    frames, rows, cols = sizes
    g, me = lax.axis_index("groups"), lax.axis_index("frame")
    r, c = lax.axis_index("row"), lax.axis_index("col")
    tile_rows, tile_cols = dark.shape
    h = c * frames + me

    def inside(i, size):
        return (i >= 0) & (i < size)

    def tile_ok(dr, dc):
        return inside(r + dr, rows) & inside(c + dc, cols)

    def strip_ok(dr, dh):
        return inside(r + dr, rows) & inside(h + dh, cols * frames)

    def strip_device(dr, dh):
        to = h + dh
        return (g, to % frames, r + dr, to // frames)

    def peer(step):
        return (me + step) % frames

    fetches = [pltpu.make_async_copy(given[i], held[i], in_sem.at[i]) for i in range(13)]
    for i in (0, 1, 2, 3, 6, 7, 4, 5, 12, 8, 9, 10, 11):
        fetches[i].start()

    barrier = pltpu.get_barrier_semaphore()
    expected = jnp.int32(frames - 1)
    for step in range(1, frames):
        pl.semaphore_signal(barrier, inc=1, device_id=(g, peer(step), r, c), device_id_type=MESH)
    for dr, dc in AROUND:
        ok = tile_ok(dr, dc)
        expected = expected + ok.astype(jnp.int32)

        @pl.when(ok)
        def _(dr=dr, dc=dc):
            pl.semaphore_signal(
                barrier, inc=1, device_id=(g, me, r + dr, c + dc), device_id_type=MESH
            )

        if dc:
            ok = strip_ok(dr, dc)
            expected = expected + ok.astype(jnp.int32)

            @pl.when(ok)
            def _(dr=dr, dc=dc):
                pl.semaphore_signal(
                    barrier, inc=1, device_id=strip_device(dr, dc), device_id_type=MESH
                )

    for i in range(4):
        fetches[i].wait()
    flat0 = (raw[0] - dark[...]) * gain[...]
    mean = 0.5 * (pltpu.roll(flat0, 1, 1) + pltpu.roll(flat0, tile_cols - 1, 1))
    ext[RIM : RIM + tile_rows, PATCH : PATCH + tile_cols] = jnp.where(bad[...] == 1, mean, flat0)
    fetches[6].wait()
    fetches[7].wait()
    ids = levels[...]
    picked = jnp.zeros(ids.shape, jnp.float32)
    for v in range(level_table.shape[0]):
        picked = jnp.where(ids == v, level_table[v], picked)
    modes = ids.shape[1]
    coeff[...] = jnp.zeros(coeff.shape, jnp.float32)
    coeff[:, :modes] = picked
    coeff_all[me] = coeff[...]

    row_src = {0: pl.ds(RIM, tile_rows), 1: pl.ds(tile_rows, RIM), -1: pl.ds(RIM, RIM)}
    row_dst = {0: pl.ds(RIM, tile_rows), 1: pl.ds(0, RIM), -1: pl.ds(RIM + tile_rows, RIM)}
    col_src = {0: pl.ds(PATCH, tile_cols), 1: pl.ds(tile_cols, PATCH), -1: pl.ds(PATCH, PATCH)}
    col_dst = {0: pl.ds(PATCH, tile_cols), 1: pl.ds(0, PATCH), -1: pl.ds(PATCH + tile_cols, PATCH)}

    def a_copy(i):
        dr, dc = AROUND[i]
        return pltpu.make_async_remote_copy(
            src_ref=ext.at[row_src[dr], col_src[dc]],
            dst_ref=ext.at[row_dst[dr], col_dst[dc]],
            send_sem=a_send.at[i],
            recv_sem=a_recv.at[i],
            device_id=(g, me, r + dr, c + dc),
            device_id_type=MESH,
        )

    def q_copy(step, source):
        return pltpu.make_async_remote_copy(
            src_ref=coeff,
            dst_ref=coeff_all.at[source],
            send_sem=q_send.at[step],
            recv_sem=q_recv.at[source],
            device_id=(g, peer(step), r, c),
            device_id_type=MESH,
        )

    height = strips.shape[1]
    if rows == 2:
        sent = pl.ds(pl.multiple_of(HALF * (1 - r), HALF), height - HALF)
    else:
        sent = pl.ds(0, height)

    def b_copy(k, source):
        return pltpu.make_async_remote_copy(
            src_ref=stage.at[k, sent],
            dst_ref=strips.at[source, sent],
            send_sem=b_send.at[k],
            recv_sem=b_recv.at[source],
            device_id=(g, k, r, c),
            device_id_type=MESH,
        )

    def c_copy(i):
        dr, dh = AROUND[i]
        source = {
            0: pack.at[(dh + 1) // 2],
            -1: strip_s.at[pl.ds(0, HALF)],
            1: strip_s.at[pl.ds(height - HALF, HALF)],
        }[dr]
        return pltpu.make_async_remote_copy(
            src_ref=source,
            dst_ref=rims.at[i],
            send_sem=c_send.at[i],
            recv_sem=c_recv.at[i],
            device_id=strip_device(dr, dh),
            device_id_type=MESH,
        )

    pl.semaphore_wait(barrier, expected)
    for i, (dr, dc) in enumerate(AROUND):

        @pl.when(tile_ok(dr, dc))
        def _(i=i):
            a_copy(i).start()

    for step in range(1, frames):
        q_copy(step, me).start()

    for i, (dr, dc) in enumerate(AROUND):

        @pl.when(jnp.logical_not(tile_ok(-dr, -dc)))
        def _(dr=dr, dc=dc):
            y, x = row_dst[dr], col_dst[dc]
            ext[y, x] = jnp.zeros((y.size, x.size), jnp.float32)

        @pl.when(jnp.logical_not(strip_ok(-dr, -dc)))
        def _(i=i):
            rims[i] = jnp.zeros(rims.shape[1:], jnp.float32)

    lag = lax.broadcasted_iota(jnp.int32, (256, PATCH), 0) - lax.broadcasted_iota(
        jnp.int32, (256, PATCH), 1
    )
    fetches[4].wait()
    fetches[5].wait()
    col_bands = [band(taps_col, lag.shape, lag - first) for first in (81, 17)]
    shape = (height, ext.shape[0])
    lag = lax.broadcasted_iota(jnp.int32, shape, 1) - lax.broadcasted_iota(jnp.int32, shape, 0)
    row_band = band(taps_row, shape, lag - 1)
    for i, (dr, dc) in enumerate(AROUND):

        @pl.when(tile_ok(-dr, -dc))
        def _(i=i):
            a_copy(i).wait_recv()

    shape = (height, PATCH)
    y_all = lax.broadcasted_iota(jnp.int32, shape, 0) + (r * tile_rows - HALF)
    x_all = lax.broadcasted_iota(jnp.int32, shape, 1) + (c * tile_cols - HALF)
    wide = ext[...]
    light = halves(dot3(row_band, halves(wide)))
    wide = wide[16 : 16 + height]
    for k in range(frames):
        first = (STEP * k + 81) // PATCH * PATCH
        part = slice(first, first + 256)
        stray = dot3([half[:, part] for half in light], col_bands[k % 2])
        at = STEP * k + 96 - first
        here = pltpu.roll(wide[:, part], 256 - at, 1)[:, :PATCH]
        x_here = x_all + STEP * k
        keep = inside(y_all, rows * tile_rows) & inside(x_here, cols * tile_cols)
        stage[k] = jnp.where(keep, here - stray, 0.0)

        @pl.when(k != me)
        def _(k=k):
            b_copy(k, me).start()

    strips[me] = stage[me]
    if rows == 2:
        edge = pl.ds(pl.multiple_of((height - HALF) * r, HALF), HALF)
        for step in range(1, frames):
            strips[peer(step), edge, :] = jnp.zeros((HALF, PATCH), jnp.float32)

    for i in (12, 8, 9, 10, 11):
        fetches[i].wait()
    y_at = lax.broadcasted_iota(jnp.int32, (PATCH, PATCH), 0)
    x_at = lax.broadcasted_iota(jnp.int32, (PATCH, PATCH), 1)
    flip = ((y_at + x_at) % PATCH == 0).astype(jnp.float32).astype(jnp.bfloat16)
    n_high, n_low = halves(noise[...])
    turned = dot(flip, n_high), dot(flip, n_low)
    turned = dot(turned[0].astype(jnp.bfloat16), flip) + dot(turned[1].astype(jnp.bfloat16), flip)
    noises = (noise[:KEPT, :], turned[:KEPT, :])
    weights = []
    for a in range(2):
        chosen = apod[a, me]
        line = jnp.zeros((1, PATCH), jnp.float32)
        for v in range(window_table.shape[0]):
            line = jnp.where(chosen == v, window_table[v : v + 1, :], line)
        column = jnp.sum(jnp.where(y_at == x_at, line, 0.0), axis=1, keepdims=True)
        weights.append(column * line)
    basis_parts = halves(basis[...])

    px = [tuple(table[i, 256 * q : 256 * q + 256, :] for i in range(2)) for q in range(2)]
    ac = tuple(table[i, 512:768, :] for i in range(2))
    bx = tuple(table[i, 768:1024, :] for i in range(2))
    py = tuple(table[i, 1024:1280, :PATCH] for i in range(2))
    fr = tuple(table[i, 1024 : 1024 + 2 * KEPT, PATCH:] for i in range(2))
    by = tuple(table[i, 1280 : 1280 + PATCH, : 2 * KEPT] for i in range(2))
    for step in range(1, frames):
        q_copy(step, peer(step)).wait_recv()
    count = 2 * frames
    mine = [
        coeff_all[peer(step), pl.ds(a * frames + me, 1), :]
        for step in range(frames)
        for a in range(2)
    ]
    phase = dot3(halves(jnp.concatenate(mine, axis=0)[:, :modes]), basis_parts)
    lines = PUPIL // 2
    for j in range(lines):
        phase_s[pl.ds(j, count, stride=lines), :] = phase[:, j * PATCH : (j + 1) * PATCH]
    y2 = 2 * (2 * y_at[:lines] + x_at[:lines] // PUPIL) - (PUPIL - 1)
    x2 = 2 * (x_at[:lines] % PUPIL) - (PUPIL - 1)
    stop = (y2 * y2 + x2 * x2 <= PUPIL * PUPIL).astype(jnp.float32)
    stop = jnp.concatenate([stop] * count, axis=0)
    real, imag = cos_sin(phase_s[...])
    field = jnp.concatenate([real * stop, imag * stop], axis=1)
    field = halves(field)
    field = [dot3(field, px[q]) for q in range(2)]
    picks = []
    for p in range(count):
        part = [field[q][p * lines : (p + 1) * lines] for q in range(2)]
        picks.append(
            jnp.concatenate(
                [part[0][:, :PATCH], part[1][:, :PATCH], part[0][:, PATCH:], part[1][:, PATCH:]],
                axis=0,
            )
        )

    def spectrum(images):
        first = dot3(fr, halves(jnp.concatenate(images, axis=1)))
        parts = [
            jnp.concatenate(
                [
                    first[:KEPT, i * PATCH : (i + 1) * PATCH],
                    first[KEPT:, i * PATCH : (i + 1) * PATCH],
                ],
                axis=1,
            )
            for i in range(len(images))
        ]
        return dot3(halves(jnp.concatenate(parts, axis=0)), ac)

    optics = []
    for step in range(frames):
        pair = jnp.concatenate(picks[2 * step : 2 * step + 2], axis=1)
        spread = dot3(py, halves(pair))
        power = spread[:PATCH] * spread[:PATCH] + spread[PATCH:] * spread[PATCH:]
        images = []
        for a in range(2):
            one = power[:, a * PATCH : (a + 1) * PATCH]
            images.append(one * (1.0 / jnp.sum(one, axis=(0, 1), keepdims=True)))
        optics.append(spectrum(images))

    totals = [[jnp.zeros((KEPT, PATCH), jnp.float32)] * 3 for a in range(2)]
    for step in range(frames):
        if step:
            b_copy(peer(step), peer(step)).wait_recv()
        images = [
            strips[peer(step), a * STEP : a * STEP + PATCH, :] * weights[a] for a in range(2)
        ]
        image = spectrum(images)
        for a in range(2):
            lot = slice(a * KEPT, (a + 1) * KEPT)
            i_re, i_im = image[lot, :PATCH], image[lot, PATCH:]
            o_re, o_im = optics[step][lot, :PATCH], optics[step][lot, PATCH:]
            total = totals[a]
            totals[a] = [
                total[0] + o_re * i_re + o_im * i_im,
                total[1] + o_re * i_im - o_im * i_re,
                total[2] + o_re * o_re + o_im * o_im,
            ]

    whole = []
    for a in range(2):
        num_re, num_im, power = totals[a]
        factor = 0.5 / (power + noises[0]) + 0.5 / (power + noises[1])
        whole.append(jnp.concatenate([num_re * factor, num_im * factor], axis=1))
    turned = dot3(halves(jnp.concatenate(whole, axis=0)), bx)
    sides = [
        jnp.concatenate(
            [turned[a * KEPT : (a + 1) * KEPT, :PATCH], turned[a * KEPT : (a + 1) * KEPT, PATCH:]],
            axis=0,
        )
        for a in range(2)
    ]
    contrib = dot3(by, halves(jnp.concatenate(sides, axis=1)))
    upper, lower = contrib[:, :PATCH], contrib[:, PATCH:]
    strip = jnp.concatenate([upper[:STEP], upper[STEP:] + lower[:STEP], lower[STEP:]], axis=0)
    strip_s[...] = strip
    body = strip[HALF : HALF + tile_rows]
    lane = lax.broadcasted_iota(jnp.int32, (HALF, PATCH), 1)
    for side in range(2):
        packed = jnp.zeros((HALF, PATCH), jnp.float32)
        for q in range(4):
            shift = (HALF * q + HALF * side) % PATCH
            rolled = body[q * HALF : (q + 1) * HALF]
            if shift:
                rolled = pltpu.roll(rolled, shift, 1)
            packed = jnp.where(lane // HALF == q, rolled, packed)
        pack[side] = packed
    for i, (dr, dh) in enumerate(AROUND):

        @pl.when(strip_ok(dr, dh))
        def _(i=i):
            c_copy(i).start()

    for i, (dr, dc) in enumerate(AROUND):

        @pl.when(tile_ok(dr, dc))
        def _(i=i):
            a_copy(i).wait_send()

    for step in range(1, frames):
        q_copy(step, me).wait_send()
        b_copy(peer(step), me).wait_send()

    for i, (dr, dh) in enumerate(AROUND):

        @pl.when(strip_ok(-dr, -dh))
        def _(i=i):
            c_copy(i).wait_recv()

    from_left, from_right = lane // HALF == 1, lane // HALF == 2
    blocks = []
    for q in range(4):
        value = body[q * HALF : (q + 1) * HALF]
        for i, (dr, dh) in enumerate(AROUND):
            if dr == 0:
                goal = 1 if dh == 1 else 2
                shift = (HALF * (goal - q)) % PATCH
                got = pltpu.roll(rims[i], shift, 1) if shift else rims[i]
                value = value + jnp.where(from_left if dh == 1 else from_right, got, 0.0)
            elif (dr == 1 and q == 0) or (dr == -1 and q == 3):
                if dh == 0:
                    value = value + rims[i]
                else:
                    got = pltpu.roll(rims[i], STEP, 1)
                    value = value + jnp.where(from_left if dh == 1 else from_right, got, 0.0)
        blocks.append(pltpu.roll(value, PATCH - HALF, 1)[:, :STEP])
    out[...] = jnp.concatenate(blocks, axis=0)

    for i, (dr, dh) in enumerate(AROUND):

        @pl.when(strip_ok(dr, dh))
        def _(i=i):
            c_copy(i).wait_send()


def per_device(
    sizes,
    raw, dark, gain, bad, taps_col, taps_row, levels, level_table, basis, apod_index, window_table, noise,
):
    frames = sizes[0]
    tile_rows, tile_cols = dark.shape
    height = tile_rows + STEP
    count = 2 * frames
    vmem = pl.BlockSpec(memory_space=pltpu.VMEM)
    operands = [
        raw, dark, gain, bad, taps_col, taps_row,
        levels.reshape(count, levels.shape[3]),
        level_table, basis, apod_index, window_table, noise,
        jnp.asarray(tables()),
    ]
    held = [
        (pltpu.SMEM if i in (4, 5, 7, 9) else pltpu.VMEM)(operand.shape, operand.dtype)
        for i, operand in enumerate(operands)
    ]
    dma = pltpu.SemaphoreType.DMA
    restored = pl.pallas_call(
        functools.partial(kernel, sizes),
        out_shape=jax.ShapeDtypeStruct((tile_rows, STEP), jnp.float32),
        in_specs=[pl.BlockSpec(memory_space=pltpu.HBM)] * 13,
        out_specs=vmem,
        scratch_shapes=held
        + [
            pltpu.VMEM((tile_rows + 2 * RIM, tile_cols + 2 * PATCH), jnp.float32),
            pltpu.VMEM((count, PATCH), jnp.float32),
            pltpu.VMEM((frames, count, PATCH), jnp.float32),
            pltpu.VMEM((count * PUPIL // 2, PATCH), jnp.float32),
            pltpu.VMEM((frames, height, PATCH), jnp.float32),
            pltpu.VMEM((frames, height, PATCH), jnp.float32),
            pltpu.VMEM((height, PATCH), jnp.float32),
            pltpu.VMEM((2, HALF, PATCH), jnp.float32),
            pltpu.VMEM((8, HALF, PATCH), jnp.float32),
            dma((8,)),
            dma((8,)),
            dma((frames,)),
            dma((frames,)),
            dma((frames,)),
            dma((frames,)),
            dma((8,)),
            dma((8,)),
            dma((13,)),
        ],
        compiler_params=pltpu.CompilerParams(
            collective_id=0, has_side_effects=True, vmem_limit_bytes=48 * 1024 * 1024
        ),
    )(*operands)
    return restored[:, None, :]


def solution(mesh):
    placed = (
        P(("groups", "frame"), "row", "col"),
        P("row", "col"),
        P("row", "col"),
        P("row", "col"),
        P(),
        P(),
        P(("groups", "frame"), "row", "col", None),
        P(),
        P(),
        P("row", "col"),
        P(),
        P(),
    )
    sizes = (mesh.shape["frame"], mesh.shape["row"], mesh.shape["col"])
    return jax.shard_map(
        functools.partial(per_device, sizes),
        mesh=mesh,
        in_specs=placed,
        out_specs=P(("groups", "row"), "col", "frame"),
        check_vma=False,
    )
```

```python
import functools
import math

import jax
import jax.numpy as jnp
import ml_dtypes
import numpy as np
from jax import lax
from jax.experimental import pallas as pl
from jax.experimental.pallas import tpu as pltpu
from jax.sharding import PartitionSpec as P

PATCH = 128
PUPIL = 64
STEP = 64
HALF = 32
RIM = 48
KEPT = 72
MESH = pl.DeviceIdType.MESH
AROUND = [(i, j) for i in (-1, 0, 1) for j in (-1, 0, 1) if (i, j) != (0, 0)]


def split_table(table):
    table = table.astype(np.float32)
    high = table.astype(ml_dtypes.bfloat16)
    return high, (table - high.astype(np.float32)).astype(ml_dtypes.bfloat16)


def tables():
    n = PATCH
    turn = np.outer(np.arange(n), np.arange(n)) % n * (2.0 * math.pi / n)
    cosine, sine = np.cos(turn), np.sin(turn)
    blend = np.sin(math.pi * (np.arange(n) + 0.5) / n) ** 2
    pupil_x = np.zeros((2, 2, PUPIL, 2, 2, n))
    for q in range(2):
        pupil_x[0, q, :, q, 0] = cosine[:PUPIL]
        pupil_x[0, q, :, q, 1] = -sine[:PUPIL]
        pupil_x[1, q, :, q, 0] = sine[:PUPIL]
        pupil_x[1, q, :, q, 1] = cosine[:PUPIL]
    order = np.array([2 * j + q for q in range(2) for j in range(PUPIL // 2)])
    c, s = cosine[:, order], sine[:, order]
    pupil_y = np.block([[c, s], [-s, c]])
    half = n // 2 + 1
    front = np.zeros((2 * KEPT, n))
    front[:half] = cosine[:half]
    front[KEPT : KEPT + half] = sine[:half]
    across = np.block([[cosine, -sine], [-sine, -cosine]])
    back_x = np.block([[cosine, sine], [-sine, cosine]]) * np.tile(blend, 2)[None, :]
    weight = np.where((np.arange(half) % (n // 2)) == 0, 1.0, 2.0) / (n * n)
    back_y = np.zeros((n, 2 * KEPT))
    back_y[:, :half] = cosine[:, :half] * weight * blend[:, None]
    back_y[:, KEPT : KEPT + half] = -sine[:, :half] * weight * blend[:, None]
    pupil_x = pupil_x.reshape(256, 2, 256)
    side = np.zeros((256, 256))
    side[:, :n] = pupil_y
    side[: 2 * KEPT, n:] = front
    last = np.zeros((n, 256))
    last[:, : 2 * KEPT] = back_y
    whole = [pupil_x[:, 0], pupil_x[:, 1], across, back_x, side, last]
    return np.stack(split_table(np.concatenate(whole, axis=0)))


def halves(value):
    high = value.astype(jnp.bfloat16)
    return high, (value - high.astype(jnp.float32)).astype(jnp.bfloat16)


def dot(left, right):
    return jnp.dot(left, right, preferred_element_type=jnp.float32)


def dot3(left, right):
    return dot(left[0], right[0]) + (dot(left[1], right[0]) + dot(left[0], right[1]))


def cos_sin(angle):
    quarter = jnp.floor(angle * (2.0 / math.pi) + 0.5)
    rest = (angle - quarter * 1.5703125) - quarter * (math.pi / 2 - 1.5703125)
    sq = rest * rest
    s = rest + rest * sq * (-1 / 6 + sq * (1 / 120 + sq * (-1 / 5040 + sq * (1 / 362880))))
    c = 1.0 + sq * (-0.5 + sq * (1 / 24 + sq * (-1 / 720 + sq * (1 / 40320))))
    turn = quarter.astype(jnp.int32) & 3
    odd = (turn & 1) == 1
    cos_value, sin_value = jnp.where(odd, s, c), jnp.where(odd, c, s)
    return (
        jnp.where((turn == 1) | (turn == 2), -cos_value, cos_value),
        jnp.where(turn >= 2, -sin_value, sin_value),
    )


def band(taps, shape, lag):
    matrix = jnp.zeros(shape, jnp.float32)
    for t in range(taps.shape[0]):
        matrix = jnp.where(lag == t, taps[t], matrix)
    return halves(matrix)


def kernel(
    sizes,
    *refs,
):
    given, refs = refs[:13], refs[13:]
    out, held, refs = refs[0], refs[1:14], refs[14:]
    (raw, dark, gain, bad, taps_col, taps_row, levels, level_table, basis, apod, window_table, noise,
     table) = held
    (ext, coeff, coeff_all, phase_s, stage, strips, strip_s, pack, rims,
     a_send, a_recv, q_send, q_recv, b_send, b_recv, c_send, c_recv, in_sem) = refs
    frames, rows, cols = sizes
    g, me = lax.axis_index("groups"), lax.axis_index("frame")
    r, c = lax.axis_index("row"), lax.axis_index("col")
    tile_rows, tile_cols = dark.shape
    h = c * frames + me

    def inside(i, size):
        return (i >= 0) & (i < size)

    def tile_ok(dr, dc):
        return inside(r + dr, rows) & inside(c + dc, cols)

    def strip_ok(dr, dh):
        return inside(r + dr, rows) & inside(h + dh, cols * frames)

    def strip_device(dr, dh):
        to = h + dh
        return (g, to % frames, r + dr, to // frames)

    def peer(step):
        return (me + step) % frames

    fetches = [pltpu.make_async_copy(given[i], held[i], in_sem.at[i]) for i in range(13)]
    for i in (0, 1, 2, 3, 6, 7, 4, 5, 12, 8, 9, 10, 11):
        fetches[i].start()

    barrier = pltpu.get_barrier_semaphore()
    expected = jnp.int32(frames - 1)
    for step in range(1, frames):
        pl.semaphore_signal(barrier, inc=1, device_id=(g, peer(step), r, c), device_id_type=MESH)
    for dr, dc in AROUND:
        ok = tile_ok(dr, dc)
        expected = expected + ok.astype(jnp.int32)

        @pl.when(ok)
        def _(dr=dr, dc=dc):
            pl.semaphore_signal(
                barrier, inc=1, device_id=(g, me, r + dr, c + dc), device_id_type=MESH
            )

        if dc:
            ok = strip_ok(dr, dc)
            expected = expected + ok.astype(jnp.int32)

            @pl.when(ok)
            def _(dr=dr, dc=dc):
                pl.semaphore_signal(
                    barrier, inc=1, device_id=strip_device(dr, dc), device_id_type=MESH
                )

    for i in range(4):
        fetches[i].wait()
    flat0 = (raw[0] - dark[...]) * gain[...]
    mean = 0.5 * (pltpu.roll(flat0, 1, 1) + pltpu.roll(flat0, tile_cols - 1, 1))
    ext[RIM : RIM + tile_rows, PATCH : PATCH + tile_cols] = jnp.where(bad[...] == 1, mean, flat0)
    fetches[6].wait()
    fetches[7].wait()
    ids = levels[...]
    picked = jnp.zeros(ids.shape, jnp.float32)
    for v in range(level_table.shape[0]):
        picked = jnp.where(ids == v, level_table[v], picked)
    modes = ids.shape[1]
    coeff[...] = jnp.zeros(coeff.shape, jnp.float32)
    coeff[:, :modes] = picked
    coeff_all[me] = coeff[...]

    row_src = {0: pl.ds(RIM, tile_rows), 1: pl.ds(tile_rows, RIM), -1: pl.ds(RIM, RIM)}
    row_dst = {0: pl.ds(RIM, tile_rows), 1: pl.ds(0, RIM), -1: pl.ds(RIM + tile_rows, RIM)}
    col_src = {0: pl.ds(PATCH, tile_cols), 1: pl.ds(tile_cols, PATCH), -1: pl.ds(PATCH, PATCH)}
    col_dst = {0: pl.ds(PATCH, tile_cols), 1: pl.ds(0, PATCH), -1: pl.ds(PATCH + tile_cols, PATCH)}

    def a_copy(i):
        dr, dc = AROUND[i]
        return pltpu.make_async_remote_copy(
            src_ref=ext.at[row_src[dr], col_src[dc]],
            dst_ref=ext.at[row_dst[dr], col_dst[dc]],
            send_sem=a_send.at[i],
            recv_sem=a_recv.at[i],
            device_id=(g, me, r + dr, c + dc),
            device_id_type=MESH,
        )

    def q_copy(step, source):
        return pltpu.make_async_remote_copy(
            src_ref=coeff,
            dst_ref=coeff_all.at[source],
            send_sem=q_send.at[step],
            recv_sem=q_recv.at[source],
            device_id=(g, peer(step), r, c),
            device_id_type=MESH,
        )

    height = strips.shape[1]
    if rows == 2:
        sent = pl.ds(pl.multiple_of(HALF * (1 - r), HALF), height - HALF)
    else:
        sent = pl.ds(0, height)

    def b_copy(k, source):
        return pltpu.make_async_remote_copy(
            src_ref=stage.at[k, sent],
            dst_ref=strips.at[source, sent],
            send_sem=b_send.at[k],
            recv_sem=b_recv.at[source],
            device_id=(g, k, r, c),
            device_id_type=MESH,
        )

    def c_copy(i):
        dr, dh = AROUND[i]
        source = {
            0: pack.at[(dh + 1) // 2],
            -1: strip_s.at[pl.ds(0, HALF)],
            1: strip_s.at[pl.ds(height - HALF, HALF)],
        }[dr]
        return pltpu.make_async_remote_copy(
            src_ref=source,
            dst_ref=rims.at[i],
            send_sem=c_send.at[i],
            recv_sem=c_recv.at[i],
            device_id=strip_device(dr, dh),
            device_id_type=MESH,
        )

    pl.semaphore_wait(barrier, expected)
    for i, (dr, dc) in enumerate(AROUND):

        @pl.when(tile_ok(dr, dc))
        def _(i=i):
            a_copy(i).start()

    for step in range(1, frames):
        q_copy(step, me).start()

    for i, (dr, dc) in enumerate(AROUND):

        @pl.when(jnp.logical_not(tile_ok(-dr, -dc)))
        def _(dr=dr, dc=dc):
            y, x = row_dst[dr], col_dst[dc]
            ext[y, x] = jnp.zeros((y.size, x.size), jnp.float32)

        @pl.when(jnp.logical_not(strip_ok(-dr, -dc)))
        def _(i=i):
            rims[i] = jnp.zeros(rims.shape[1:], jnp.float32)

    lag = lax.broadcasted_iota(jnp.int32, (256, PATCH), 0) - lax.broadcasted_iota(
        jnp.int32, (256, PATCH), 1
    )
    fetches[4].wait()
    fetches[5].wait()
    col_bands = [band(taps_col, lag.shape, lag - first) for first in (81, 17)]
    shape = (height, ext.shape[0])
    lag = lax.broadcasted_iota(jnp.int32, shape, 1) - lax.broadcasted_iota(jnp.int32, shape, 0)
    row_band = band(taps_row, shape, lag - 1)
    for i, (dr, dc) in enumerate(AROUND):

        @pl.when(tile_ok(-dr, -dc))
        def _(i=i):
            a_copy(i).wait_recv()

    shape = (height, PATCH)
    y_all = lax.broadcasted_iota(jnp.int32, shape, 0) + (r * tile_rows - HALF)
    x_all = lax.broadcasted_iota(jnp.int32, shape, 1) + (c * tile_cols - HALF)
    wide = ext[...]
    light = halves(dot3(row_band, halves(wide)))
    wide = wide[16 : 16 + height]
    for k in range(frames):
        first = (STEP * k + 81) // PATCH * PATCH
        part = slice(first, first + 256)
        stray = dot3([half[:, part] for half in light], col_bands[k % 2])
        at = STEP * k + 96 - first
        here = pltpu.roll(wide[:, part], 256 - at, 1)[:, :PATCH]
        x_here = x_all + STEP * k
        keep = inside(y_all, rows * tile_rows) & inside(x_here, cols * tile_cols)
        stage[k] = jnp.where(keep, here - stray, 0.0)

        @pl.when(k != me)
        def _(k=k):
            b_copy(k, me).start()

    strips[me] = stage[me]
    if rows == 2:
        edge = pl.ds(pl.multiple_of((height - HALF) * r, HALF), HALF)
        for step in range(1, frames):
            strips[peer(step), edge, :] = jnp.zeros((HALF, PATCH), jnp.float32)

    for i in (12, 8, 9, 10, 11):
        fetches[i].wait()
    y_at = lax.broadcasted_iota(jnp.int32, (PATCH, PATCH), 0)
    x_at = lax.broadcasted_iota(jnp.int32, (PATCH, PATCH), 1)
    flip = ((y_at + x_at) % PATCH == 0).astype(jnp.float32).astype(jnp.bfloat16)
    n_high, n_low = halves(noise[...])
    turned = dot(flip, n_high), dot(flip, n_low)
    turned = dot(turned[0].astype(jnp.bfloat16), flip) + dot(turned[1].astype(jnp.bfloat16), flip)
    noises = (noise[:KEPT, :], turned[:KEPT, :])
    weights = []
    for a in range(2):
        chosen = apod[a, me]
        line = jnp.zeros((1, PATCH), jnp.float32)
        for v in range(window_table.shape[0]):
            line = jnp.where(chosen == v, window_table[v : v + 1, :], line)
        column = jnp.sum(jnp.where(y_at == x_at, line, 0.0), axis=1, keepdims=True)
        weights.append(column * line)
    basis_parts = halves(basis[...])

    px = [tuple(table[i, 256 * q : 256 * q + 256, :] for i in range(2)) for q in range(2)]
    ac = tuple(table[i, 512:768, :] for i in range(2))
    bx = tuple(table[i, 768:1024, :] for i in range(2))
    py = tuple(table[i, 1024:1280, :PATCH] for i in range(2))
    fr = tuple(table[i, 1024 : 1024 + 2 * KEPT, PATCH:] for i in range(2))
    by = tuple(table[i, 1280 : 1280 + PATCH, : 2 * KEPT] for i in range(2))
    for step in range(1, frames):
        q_copy(step, peer(step)).wait_recv()
    count = 2 * frames
    mine = [
        coeff_all[peer(step), pl.ds(a * frames + me, 1), :]
        for step in range(frames)
        for a in range(2)
    ]
    phase = dot3(halves(jnp.concatenate(mine, axis=0)[:, :modes]), basis_parts)
    lines = PUPIL // 2
    for j in range(lines):
        phase_s[pl.ds(j, count, stride=lines), :] = phase[:, j * PATCH : (j + 1) * PATCH]
    y2 = 2 * (2 * y_at[:lines] + x_at[:lines] // PUPIL) - (PUPIL - 1)
    x2 = 2 * (x_at[:lines] % PUPIL) - (PUPIL - 1)
    stop = (y2 * y2 + x2 * x2 <= PUPIL * PUPIL).astype(jnp.float32)
    stop = jnp.concatenate([stop] * count, axis=0)
    real, imag = cos_sin(phase_s[...])
    field = jnp.concatenate([real * stop, imag * stop], axis=1)
    field = halves(field)
    field = [dot3(field, px[q]) for q in range(2)]
    picks = []
    for p in range(count):
        part = [field[q][p * lines : (p + 1) * lines] for q in range(2)]
        picks.append(
            jnp.concatenate(
                [part[0][:, :PATCH], part[1][:, :PATCH], part[0][:, PATCH:], part[1][:, PATCH:]],
                axis=0,
            )
        )

    def spectrum(images):
        first = dot3(fr, halves(jnp.concatenate(images, axis=1)))
        parts = [
            jnp.concatenate(
                [
                    first[:KEPT, i * PATCH : (i + 1) * PATCH],
                    first[KEPT:, i * PATCH : (i + 1) * PATCH],
                ],
                axis=1,
            )
            for i in range(len(images))
        ]
        return dot3(halves(jnp.concatenate(parts, axis=0)), ac)

    optics = []
    for step in range(frames):
        pair = jnp.concatenate(picks[2 * step : 2 * step + 2], axis=1)
        spread = dot3(py, halves(pair))
        power = spread[:PATCH] * spread[:PATCH] + spread[PATCH:] * spread[PATCH:]
        images = []
        for a in range(2):
            one = power[:, a * PATCH : (a + 1) * PATCH]
            images.append(one * (1.0 / jnp.sum(one, axis=(0, 1), keepdims=True)))
        optics.append(spectrum(images))

    totals = [[jnp.zeros((KEPT, PATCH), jnp.float32)] * 3 for a in range(2)]
    for step in range(frames):
        if step:
            b_copy(peer(step), peer(step)).wait_recv()
        images = [
            strips[peer(step), a * STEP : a * STEP + PATCH, :] * weights[a] for a in range(2)
        ]
        image = spectrum(images)
        for a in range(2):
            lot = slice(a * KEPT, (a + 1) * KEPT)
            i_re, i_im = image[lot, :PATCH], image[lot, PATCH:]
            o_re, o_im = optics[step][lot, :PATCH], optics[step][lot, PATCH:]
            total = totals[a]
            totals[a] = [
                total[0] + o_re * i_re + o_im * i_im,
                total[1] + o_re * i_im - o_im * i_re,
                total[2] + o_re * o_re + o_im * o_im,
            ]

    whole = []
    for a in range(2):
        num_re, num_im, power = totals[a]
        factor = 0.5 / (power + noises[0]) + 0.5 / (power + noises[1])
        whole.append(jnp.concatenate([num_re * factor, num_im * factor], axis=1))
    turned = dot3(halves(jnp.concatenate(whole, axis=0)), bx)
    sides = [
        jnp.concatenate(
            [turned[a * KEPT : (a + 1) * KEPT, :PATCH], turned[a * KEPT : (a + 1) * KEPT, PATCH:]],
            axis=0,
        )
        for a in range(2)
    ]
    contrib = dot3(by, halves(jnp.concatenate(sides, axis=1)))
    upper, lower = contrib[:, :PATCH], contrib[:, PATCH:]
    strip = jnp.concatenate([upper[:STEP], upper[STEP:] + lower[:STEP], lower[STEP:]], axis=0)
    strip_s[...] = strip
    body = strip[HALF : HALF + tile_rows]
    lane = lax.broadcasted_iota(jnp.int32, (HALF, PATCH), 1)
    for side in range(2):
        packed = jnp.zeros((HALF, PATCH), jnp.float32)
        for q in range(4):
            shift = (HALF * q + HALF * side) % PATCH
            rolled = body[q * HALF : (q + 1) * HALF]
            if shift:
                rolled = pltpu.roll(rolled, shift, 1)
            packed = jnp.where(lane // HALF == q, rolled, packed)
        pack[side] = packed
    for i, (dr, dh) in enumerate(AROUND):

        @pl.when(strip_ok(dr, dh))
        def _(i=i):
            c_copy(i).start()

    for i, (dr, dc) in enumerate(AROUND):

        @pl.when(tile_ok(dr, dc))
        def _(i=i):
            a_copy(i).wait_send()

    for step in range(1, frames):
        q_copy(step, me).wait_send()
        b_copy(peer(step), me).wait_send()

    for i, (dr, dh) in enumerate(AROUND):

        @pl.when(strip_ok(-dr, -dh))
        def _(i=i):
            c_copy(i).wait_recv()

    from_left, from_right = lane // HALF == 1, lane // HALF == 2
    blocks = []
    for q in range(4):
        value = body[q * HALF : (q + 1) * HALF]
        for i, (dr, dh) in enumerate(AROUND):
            if dr == 0:
                goal = 1 if dh == 1 else 2
                shift = (HALF * (goal - q)) % PATCH
                got = pltpu.roll(rims[i], shift, 1) if shift else rims[i]
                value = value + jnp.where(from_left if dh == 1 else from_right, got, 0.0)
            elif (dr == 1 and q == 0) or (dr == -1 and q == 3):
                if dh == 0:
                    value = value + rims[i]
                else:
                    got = pltpu.roll(rims[i], STEP, 1)
                    value = value + jnp.where(from_left if dh == 1 else from_right, got, 0.0)
        blocks.append(value)
    out[...] = jnp.concatenate(blocks, axis=0).T[HALF : HALF + STEP, :]

    for i, (dr, dh) in enumerate(AROUND):

        @pl.when(strip_ok(dr, dh))
        def _(i=i):
            c_copy(i).wait_send()


def per_device(
    sizes,
    raw, dark, gain, bad, taps_col, taps_row, levels, level_table, basis, apod_index, window_table, noise,
):
    frames = sizes[0]
    tile_rows, tile_cols = dark.shape
    height = tile_rows + STEP
    count = 2 * frames
    vmem = pl.BlockSpec(memory_space=pltpu.VMEM)
    operands = [
        raw, dark, gain, bad, taps_col, taps_row,
        levels.reshape(count, levels.shape[3]),
        level_table, basis, apod_index, window_table, noise,
        jnp.asarray(tables()),
    ]
    held = [
        (pltpu.SMEM if i in (4, 5, 7, 9) else pltpu.VMEM)(operand.shape, operand.dtype)
        for i, operand in enumerate(operands)
    ]
    dma = pltpu.SemaphoreType.DMA
    restored = pl.pallas_call(
        functools.partial(kernel, sizes),
        out_shape=jax.ShapeDtypeStruct((STEP, tile_rows), jnp.float32),
        in_specs=[pl.BlockSpec(memory_space=pltpu.HBM)] * 13,
        out_specs=vmem,
        scratch_shapes=held
        + [
            pltpu.VMEM((tile_rows + 2 * RIM, tile_cols + 2 * PATCH), jnp.float32),
            pltpu.VMEM((count, PATCH), jnp.float32),
            pltpu.VMEM((frames, count, PATCH), jnp.float32),
            pltpu.VMEM((count * PUPIL // 2, PATCH), jnp.float32),
            pltpu.VMEM((frames, height, PATCH), jnp.float32),
            pltpu.VMEM((frames, height, PATCH), jnp.float32),
            pltpu.VMEM((height, PATCH), jnp.float32),
            pltpu.VMEM((2, HALF, PATCH), jnp.float32),
            pltpu.VMEM((8, HALF, PATCH), jnp.float32),
            dma((8,)),
            dma((8,)),
            dma((frames,)),
            dma((frames,)),
            dma((frames,)),
            dma((frames,)),
            dma((8,)),
            dma((8,)),
            dma((13,)),
        ],
        compiler_params=pltpu.CompilerParams(
            collective_id=0, has_side_effects=True, vmem_limit_bytes=64 * 1024 * 1024
        ),
    )(*operands)
    return restored.T[:, None, :]


def solution(mesh):
    placed = (
        P(("groups", "frame"), "row", "col"),
        P("row", "col"),
        P("row", "col"),
        P("row", "col"),
        P(),
        P(),
        P(("groups", "frame"), "row", "col", None),
        P(),
        P(),
        P("row", "col"),
        P(),
        P(),
    )
    sizes = (mesh.shape["frame"], mesh.shape["row"], mesh.shape["col"])
    return jax.shard_map(
        functools.partial(per_device, sizes),
        mesh=mesh,
        in_specs=placed,
        out_specs=P(("groups", "row"), "col", "frame"),
        check_vma=False,
    )
```

```python
import functools
import math

import jax
import jax.numpy as jnp
import ml_dtypes
import numpy as np
from jax import lax
from jax.experimental import pallas as pl
from jax.experimental.pallas import tpu as pltpu
from jax.sharding import PartitionSpec as P

PATCH = 128
PUPIL = 64
STEP = 64
HALF = 32
RIM = 48
KEPT = 72
MESH = pl.DeviceIdType.MESH
AROUND = [(i, j) for i in (-1, 0, 1) for j in (-1, 0, 1) if (i, j) != (0, 0)]


def split_table(table):
    table = table.astype(np.float32)
    high = table.astype(ml_dtypes.bfloat16)
    return high, (table - high.astype(np.float32)).astype(ml_dtypes.bfloat16)


def tables():
    n = PATCH
    turn = np.outer(np.arange(n), np.arange(n)) % n * (2.0 * math.pi / n)
    cosine, sine = np.cos(turn), np.sin(turn)
    blend = np.sin(math.pi * (np.arange(n) + 0.5) / n) ** 2
    pupil_x = np.zeros((2, 2, PUPIL, 2, 2, n))
    for q in range(2):
        pupil_x[0, q, :, q, 0] = cosine[:PUPIL]
        pupil_x[0, q, :, q, 1] = -sine[:PUPIL]
        pupil_x[1, q, :, q, 0] = sine[:PUPIL]
        pupil_x[1, q, :, q, 1] = cosine[:PUPIL]
    order = np.array([2 * j + q for q in range(2) for j in range(PUPIL // 2)])
    c, s = cosine[:, order], sine[:, order]
    pupil_y = np.block([[c, s], [-s, c]])
    half = n // 2 + 1
    front = np.zeros((2 * KEPT, n))
    front[:half] = cosine[:half]
    front[KEPT : KEPT + half] = sine[:half]
    across = np.block([[cosine, -sine], [-sine, -cosine]])
    back_x = np.block([[cosine, sine], [-sine, cosine]]) * np.tile(blend, 2)[None, :]
    weight = np.where((np.arange(half) % (n // 2)) == 0, 1.0, 2.0) / (n * n)
    back_y = np.zeros((n, 2 * KEPT))
    back_y[:, :half] = cosine[:, :half] * weight * blend[:, None]
    back_y[:, KEPT : KEPT + half] = -sine[:, :half] * weight * blend[:, None]
    pupil_x = pupil_x.reshape(256, 2, 256)
    side = np.zeros((256, 256))
    side[:, :n] = pupil_y
    side[: 2 * KEPT, n:] = front
    last = np.zeros((n, 256))
    last[:, : 2 * KEPT] = back_y
    whole = [pupil_x[:, 0], pupil_x[:, 1], across, back_x, side, last]
    return np.stack(split_table(np.concatenate(whole, axis=0)))


def halves(value):
    high = value.astype(jnp.bfloat16)
    return high, (value - high.astype(jnp.float32)).astype(jnp.bfloat16)


def dot(left, right):
    return jnp.dot(left, right, preferred_element_type=jnp.float32)


def dot3(left, right):
    return dot(left[0], right[0]) + (dot(left[1], right[0]) + dot(left[0], right[1]))


def cos_sin(angle):
    quarter = jnp.floor(angle * (2.0 / math.pi) + 0.5)
    rest = (angle - quarter * 1.5703125) - quarter * (math.pi / 2 - 1.5703125)
    sq = rest * rest
    s = rest + rest * sq * (-1 / 6 + sq * (1 / 120 + sq * (-1 / 5040 + sq * (1 / 362880))))
    c = 1.0 + sq * (-0.5 + sq * (1 / 24 + sq * (-1 / 720 + sq * (1 / 40320))))
    turn = quarter.astype(jnp.int32) & 3
    odd = (turn & 1) == 1
    cos_value, sin_value = jnp.where(odd, s, c), jnp.where(odd, c, s)
    return (
        jnp.where((turn == 1) | (turn == 2), -cos_value, cos_value),
        jnp.where(turn >= 2, -sin_value, sin_value),
    )


def band(taps, shape, lag):
    matrix = jnp.zeros(shape, jnp.float32)
    for t in range(taps.shape[0]):
        matrix = jnp.where(lag == t, taps[t], matrix)
    return halves(matrix)


def kernel(
    sizes,
    *refs,
):
    given, refs = refs[:13], refs[13:]
    out, held, refs = refs[0], refs[1:14], refs[14:]
    (raw, dark, gain, bad, taps_col, taps_row, levels, level_table, basis, apod, window_table, noise,
     table) = held
    (ext, coeff, coeff_all, phase_s, stage, strips, strip_s, pack, rims,
     a_send, a_recv, q_send, q_recv, b_send, b_recv, c_send, c_recv, in_sem) = refs
    frames, rows, cols = sizes
    g, me = lax.axis_index("groups"), lax.axis_index("frame")
    r, c = lax.axis_index("row"), lax.axis_index("col")
    tile_rows, tile_cols = dark.shape
    h = c * frames + me

    def inside(i, size):
        return (i >= 0) & (i < size)

    def tile_ok(dr, dc):
        return inside(r + dr, rows) & inside(c + dc, cols)

    def strip_ok(dr, dh):
        return inside(r + dr, rows) & inside(h + dh, cols * frames)

    def strip_device(dr, dh):
        to = h + dh
        return (g, to % frames, r + dr, to // frames)

    def peer(step):
        if frames & (frames - 1):
            return (me + step) % frames
        value, bit = me, 1
        while bit <= step:
            if step & bit:
                value = value + bit * (1 - 2 * ((value // bit) % 2))
            bit *= 2
        return value

    fetches = [pltpu.make_async_copy(given[i], held[i], in_sem.at[i]) for i in range(13)]
    for i in (0, 1, 2, 3, 6, 7, 4, 5, 12, 8, 9, 10, 11):
        fetches[i].start()

    barrier = pltpu.get_barrier_semaphore()
    expected = jnp.int32(frames - 1)
    for step in range(1, frames):
        pl.semaphore_signal(barrier, inc=1, device_id=(g, peer(step), r, c), device_id_type=MESH)
    for dr, dc in AROUND:
        ok = tile_ok(dr, dc)
        expected = expected + ok.astype(jnp.int32)

        @pl.when(ok)
        def _(dr=dr, dc=dc):
            pl.semaphore_signal(
                barrier, inc=1, device_id=(g, me, r + dr, c + dc), device_id_type=MESH
            )

        if dc:
            ok = strip_ok(dr, dc)
            expected = expected + ok.astype(jnp.int32)

            @pl.when(ok)
            def _(dr=dr, dc=dc):
                pl.semaphore_signal(
                    barrier, inc=1, device_id=strip_device(dr, dc), device_id_type=MESH
                )

    for i in range(4):
        fetches[i].wait()
    flat0 = (raw[0] - dark[...]) * gain[...]
    mean = 0.5 * (pltpu.roll(flat0, 1, 1) + pltpu.roll(flat0, tile_cols - 1, 1))
    ext[RIM : RIM + tile_rows, PATCH : PATCH + tile_cols] = jnp.where(bad[...] == 1, mean, flat0)
    fetches[6].wait()
    fetches[7].wait()
    ids = levels[...]
    picked = jnp.zeros(ids.shape, jnp.float32)
    for v in range(level_table.shape[0]):
        picked = jnp.where(ids == v, level_table[v], picked)
    modes = ids.shape[1]
    coeff[...] = jnp.zeros(coeff.shape, jnp.float32)
    coeff[:, :modes] = picked
    coeff_all[me] = coeff[...]

    row_src = {0: pl.ds(RIM, tile_rows), 1: pl.ds(tile_rows, RIM), -1: pl.ds(RIM, RIM)}
    row_dst = {0: pl.ds(RIM, tile_rows), 1: pl.ds(0, RIM), -1: pl.ds(RIM + tile_rows, RIM)}
    col_src = {0: pl.ds(PATCH, tile_cols), 1: pl.ds(tile_cols, PATCH), -1: pl.ds(PATCH, PATCH)}
    col_dst = {0: pl.ds(PATCH, tile_cols), 1: pl.ds(0, PATCH), -1: pl.ds(PATCH + tile_cols, PATCH)}

    def a_copy(i):
        dr, dc = AROUND[i]
        return pltpu.make_async_remote_copy(
            src_ref=ext.at[row_src[dr], col_src[dc]],
            dst_ref=ext.at[row_dst[dr], col_dst[dc]],
            send_sem=a_send.at[i],
            recv_sem=a_recv.at[i],
            device_id=(g, me, r + dr, c + dc),
            device_id_type=MESH,
        )

    def q_copy(step, source):
        return pltpu.make_async_remote_copy(
            src_ref=coeff,
            dst_ref=coeff_all.at[source],
            send_sem=q_send.at[step],
            recv_sem=q_recv.at[source],
            device_id=(g, peer(step), r, c),
            device_id_type=MESH,
        )

    height = strips.shape[1]
    if rows == 2:
        spans = [
            pl.ds(RIM, height - 2 * RIM),
            pl.ds(pl.multiple_of((height - RIM) * (1 - r), 16), RIM),
            pl.ds(pl.multiple_of(HALF + (height - RIM - HALF) * r, 16), RIM - HALF),
        ]
    else:
        spans = [pl.ds(RIM, height - 2 * RIM), pl.ds(0, RIM), pl.ds(height - RIM, RIM)]

    def b_copy(k, source, n):
        return pltpu.make_async_remote_copy(
            src_ref=stage.at[k, spans[n]],
            dst_ref=strips.at[source, spans[n]],
            send_sem=b_send.at[n, k],
            recv_sem=b_recv.at[n, source],
            device_id=(g, k, r, c),
            device_id_type=MESH,
        )

    def c_copy(i):
        dr, dh = AROUND[i]
        source = {
            0: pack.at[(dh + 1) // 2],
            -1: strip_s.at[pl.ds(0, HALF)],
            1: strip_s.at[pl.ds(height - HALF, HALF)],
        }[dr]
        return pltpu.make_async_remote_copy(
            src_ref=source,
            dst_ref=rims.at[i],
            send_sem=c_send.at[i],
            recv_sem=c_recv.at[i],
            device_id=strip_device(dr, dh),
            device_id_type=MESH,
        )

    pl.semaphore_wait(barrier, expected)
    for i, (dr, dc) in enumerate(AROUND):

        @pl.when(tile_ok(dr, dc))
        def _(i=i):
            a_copy(i).start()

    for step in range(1, frames):
        q_copy(step, me).start()

    for i, (dr, dc) in enumerate(AROUND):

        @pl.when(jnp.logical_not(tile_ok(-dr, -dc)))
        def _(dr=dr, dc=dc):
            y, x = row_dst[dr], col_dst[dc]
            ext[y, x] = jnp.zeros((y.size, x.size), jnp.float32)

        @pl.when(jnp.logical_not(strip_ok(-dr, -dc)))
        def _(i=i):
            rims[i] = jnp.zeros(rims.shape[1:], jnp.float32)

    lag = lax.broadcasted_iota(jnp.int32, (256, PATCH), 0) - lax.broadcasted_iota(
        jnp.int32, (256, PATCH), 1
    )
    fetches[4].wait()
    fetches[5].wait()
    col_bands = [band(taps_col, lag.shape, lag - first) for first in (81, 17)]
    shape = (height - 2 * RIM, tile_rows)
    lag = lax.broadcasted_iota(jnp.int32, shape, 1) - lax.broadcasted_iota(jnp.int32, shape, 0)
    row_band = band(taps_row, shape, lag - 1)
    def await_tiles(chosen):
        for i, (dr, dc) in enumerate(AROUND):
            if chosen(dr):

                @pl.when(tile_ok(-dr, -dc))
                def _(i=i):
                    a_copy(i).wait_recv()

    def correct(first, size, reach):
        light = [half[:size, :reach] for half in row_band]
        light = halves(dot3(light, halves(ext[first : first + reach, :])))
        wide = ext[first + 16 : first + 16 + size, :]
        y_here = lax.broadcasted_iota(jnp.int32, (size, PATCH), 0) + (r * tile_rows - HALF + first)
        x_here = lax.broadcasted_iota(jnp.int32, (size, PATCH), 1) + (c * tile_cols - HALF)
        for k in range(frames):
            begin = (STEP * k + 81) // PATCH * PATCH
            part = slice(begin, begin + 256)
            stray = dot3([half[:, part] for half in light], col_bands[k % 2])
            at = STEP * k + 96 - begin
            here = pltpu.roll(wide[:, part], 256 - at, 1)[:, :PATCH]
            keep = inside(y_here, rows * tile_rows) & inside(x_here + STEP * k, cols * tile_cols)
            stage[k, first : first + size, :] = jnp.where(keep, here - stray, 0.0)

    def send_spans(chosen):
        for k in range(frames):

            @pl.when(k != me)
            def _(k=k):
                for n in chosen:
                    b_copy(k, me, n).start()

    await_tiles(lambda dr: dr == 0)
    correct(RIM, height - 2 * RIM, tile_rows)
    send_spans((0,))
    await_tiles(lambda dr: dr != 0)
    correct(0, RIM, RIM + HALF)
    correct(height - RIM, RIM, RIM + HALF)
    send_spans((1, 2))
    strips[me] = stage[me]
    if rows == 2:
        edge = pl.ds(pl.multiple_of((height - HALF) * r, HALF), HALF)
        for step in range(1, frames):
            strips[peer(step), edge, :] = jnp.zeros((HALF, PATCH), jnp.float32)

    for i in (12, 8, 9, 10, 11):
        fetches[i].wait()
    y_at = lax.broadcasted_iota(jnp.int32, (PATCH, PATCH), 0)
    x_at = lax.broadcasted_iota(jnp.int32, (PATCH, PATCH), 1)
    flip = ((y_at + x_at) % PATCH == 0).astype(jnp.float32).astype(jnp.bfloat16)
    n_high, n_low = halves(noise[...])
    turned = dot(flip, n_high), dot(flip, n_low)
    turned = dot(turned[0].astype(jnp.bfloat16), flip) + dot(turned[1].astype(jnp.bfloat16), flip)
    noises = (noise[:KEPT, :], turned[:KEPT, :])
    weights = []
    for a in range(2):
        chosen = apod[a, me]
        line = jnp.zeros((1, PATCH), jnp.float32)
        for v in range(window_table.shape[0]):
            line = jnp.where(chosen == v, window_table[v : v + 1, :], line)
        column = jnp.sum(jnp.where(y_at == x_at, line, 0.0), axis=1, keepdims=True)
        weights.append(column * line)
    basis_parts = halves(basis[...])

    px = [tuple(table[i, 256 * q : 256 * q + 256, :] for i in range(2)) for q in range(2)]
    ac = tuple(table[i, 512:768, :] for i in range(2))
    bx = tuple(table[i, 768:1024, :] for i in range(2))
    py = tuple(table[i, 1024:1280, :PATCH] for i in range(2))
    fr = tuple(table[i, 1024 : 1024 + 2 * KEPT, PATCH:] for i in range(2))
    by = tuple(table[i, 1280 : 1280 + PATCH, : 2 * KEPT] for i in range(2))
    for step in range(1, frames):
        q_copy(step, peer(step)).wait_recv()
    count = 2 * frames
    mine = [
        coeff_all[peer(step), pl.ds(a * frames + me, 1), :]
        for step in range(frames)
        for a in range(2)
    ]
    phase = dot3(halves(jnp.concatenate(mine, axis=0)[:, :modes]), basis_parts)
    lines = PUPIL // 2
    for j in range(lines):
        phase_s[pl.ds(j, count, stride=lines), :] = phase[:, j * PATCH : (j + 1) * PATCH]
    y2 = 2 * (2 * y_at[:lines] + x_at[:lines] // PUPIL) - (PUPIL - 1)
    x2 = 2 * (x_at[:lines] % PUPIL) - (PUPIL - 1)
    stop = (y2 * y2 + x2 * x2 <= PUPIL * PUPIL).astype(jnp.float32)
    stop = jnp.concatenate([stop] * count, axis=0)
    real, imag = cos_sin(phase_s[...])
    field = jnp.concatenate([real * stop, imag * stop], axis=1)
    field = halves(field)
    field = [dot3(field, px[q]) for q in range(2)]
    picks = []
    for p in range(count):
        part = [field[q][p * lines : (p + 1) * lines] for q in range(2)]
        picks.append(
            jnp.concatenate(
                [part[0][:, :PATCH], part[1][:, :PATCH], part[0][:, PATCH:], part[1][:, PATCH:]],
                axis=0,
            )
        )

    def spectrum(images):
        first = dot3(fr, halves(jnp.concatenate(images, axis=1)))
        parts = [
            jnp.concatenate(
                [
                    first[:KEPT, i * PATCH : (i + 1) * PATCH],
                    first[KEPT:, i * PATCH : (i + 1) * PATCH],
                ],
                axis=1,
            )
            for i in range(len(images))
        ]
        return dot3(halves(jnp.concatenate(parts, axis=0)), ac)

    optics = []
    for step in range(frames):
        pair = jnp.concatenate(picks[2 * step : 2 * step + 2], axis=1)
        spread = dot3(py, halves(pair))
        power = spread[:PATCH] * spread[:PATCH] + spread[PATCH:] * spread[PATCH:]
        images = []
        for a in range(2):
            one = power[:, a * PATCH : (a + 1) * PATCH]
            images.append(one * (1.0 / jnp.sum(one, axis=(0, 1), keepdims=True)))
        optics.append(spectrum(images))

    totals = [[jnp.zeros((KEPT, PATCH), jnp.float32)] * 3 for a in range(2)]
    for step in range(frames):
        if step:
            for n in range(3):
                b_copy(peer(step), peer(step), n).wait_recv()
        images = [
            strips[peer(step), a * STEP : a * STEP + PATCH, :] * weights[a] for a in range(2)
        ]
        image = spectrum(images)
        for a in range(2):
            lot = slice(a * KEPT, (a + 1) * KEPT)
            i_re, i_im = image[lot, :PATCH], image[lot, PATCH:]
            o_re, o_im = optics[step][lot, :PATCH], optics[step][lot, PATCH:]
            total = totals[a]
            totals[a] = [
                total[0] + o_re * i_re + o_im * i_im,
                total[1] + o_re * i_im - o_im * i_re,
                total[2] + o_re * o_re + o_im * o_im,
            ]

    whole = []
    for a in range(2):
        num_re, num_im, power = totals[a]
        factor = 0.5 / (power + noises[0]) + 0.5 / (power + noises[1])
        whole.append(jnp.concatenate([num_re * factor, num_im * factor], axis=1))
    turned = dot3(halves(jnp.concatenate(whole, axis=0)), bx)
    sides = [
        jnp.concatenate(
            [turned[a * KEPT : (a + 1) * KEPT, :PATCH], turned[a * KEPT : (a + 1) * KEPT, PATCH:]],
            axis=0,
        )
        for a in range(2)
    ]
    contrib = dot3(by, halves(jnp.concatenate(sides, axis=1)))
    upper, lower = contrib[:, :PATCH], contrib[:, PATCH:]
    strip = jnp.concatenate([upper[:STEP], upper[STEP:] + lower[:STEP], lower[STEP:]], axis=0)
    strip_s[...] = strip
    body = strip[HALF : HALF + tile_rows]
    lane = lax.broadcasted_iota(jnp.int32, (HALF, PATCH), 1)
    for side in range(2):
        packed = jnp.zeros((HALF, PATCH), jnp.float32)
        for q in range(4):
            shift = (HALF * q + HALF * side) % PATCH
            rolled = body[q * HALF : (q + 1) * HALF]
            if shift:
                rolled = pltpu.roll(rolled, shift, 1)
            packed = jnp.where(lane // HALF == q, rolled, packed)
        pack[side] = packed
    for i, (dr, dh) in enumerate(AROUND):

        @pl.when(strip_ok(dr, dh))
        def _(i=i):
            c_copy(i).start()

    for i, (dr, dc) in enumerate(AROUND):

        @pl.when(tile_ok(dr, dc))
        def _(i=i):
            a_copy(i).wait_send()

    for step in range(1, frames):
        q_copy(step, me).wait_send()
        for n in range(3):
            b_copy(peer(step), me, n).wait_send()

    for i, (dr, dh) in enumerate(AROUND):

        @pl.when(strip_ok(-dr, -dh))
        def _(i=i):
            c_copy(i).wait_recv()

    from_left, from_right = lane // HALF == 1, lane // HALF == 2
    blocks = []
    for q in range(4):
        value = body[q * HALF : (q + 1) * HALF]
        for i, (dr, dh) in enumerate(AROUND):
            if dr == 0:
                goal = 1 if dh == 1 else 2
                shift = (HALF * (goal - q)) % PATCH
                got = pltpu.roll(rims[i], shift, 1) if shift else rims[i]
                value = value + jnp.where(from_left if dh == 1 else from_right, got, 0.0)
            elif (dr == 1 and q == 0) or (dr == -1 and q == 3):
                if dh == 0:
                    value = value + rims[i]
                else:
                    got = pltpu.roll(rims[i], STEP, 1)
                    value = value + jnp.where(from_left if dh == 1 else from_right, got, 0.0)
        blocks.append(value)
    out[...] = jnp.concatenate(blocks, axis=0).T[HALF : HALF + STEP, :]

    for i, (dr, dh) in enumerate(AROUND):

        @pl.when(strip_ok(dr, dh))
        def _(i=i):
            c_copy(i).wait_send()


def per_device(
    sizes,
    raw, dark, gain, bad, taps_col, taps_row, levels, level_table, basis, apod_index, window_table, noise,
):
    frames = sizes[0]
    tile_rows, tile_cols = dark.shape
    height = tile_rows + STEP
    count = 2 * frames
    vmem = pl.BlockSpec(memory_space=pltpu.VMEM)
    operands = [
        raw, dark, gain, bad, taps_col, taps_row,
        levels.reshape(count, levels.shape[3]),
        level_table, basis, apod_index, window_table, noise,
        jnp.asarray(tables()),
    ]
    held = [
        (pltpu.SMEM if i in (4, 5, 7, 9) else pltpu.VMEM)(operand.shape, operand.dtype)
        for i, operand in enumerate(operands)
    ]
    dma = pltpu.SemaphoreType.DMA
    restored = pl.pallas_call(
        functools.partial(kernel, sizes),
        out_shape=jax.ShapeDtypeStruct((STEP, tile_rows), jnp.float32),
        in_specs=[pl.BlockSpec(memory_space=pltpu.HBM)] * 13,
        out_specs=vmem,
        scratch_shapes=held
        + [
            pltpu.VMEM((tile_rows + 2 * RIM, tile_cols + 2 * PATCH), jnp.float32),
            pltpu.VMEM((count, PATCH), jnp.float32),
            pltpu.VMEM((frames, count, PATCH), jnp.float32),
            pltpu.VMEM((count * PUPIL // 2, PATCH), jnp.float32),
            pltpu.VMEM((frames, height, PATCH), jnp.float32),
            pltpu.VMEM((frames, height, PATCH), jnp.float32),
            pltpu.VMEM((height, PATCH), jnp.float32),
            pltpu.VMEM((2, HALF, PATCH), jnp.float32),
            pltpu.VMEM((8, HALF, PATCH), jnp.float32),
            dma((8,)),
            dma((8,)),
            dma((frames,)),
            dma((frames,)),
            dma((3, frames)),
            dma((3, frames)),
            dma((8,)),
            dma((8,)),
            dma((13,)),
        ],
        compiler_params=pltpu.CompilerParams(
            collective_id=0, has_side_effects=True, vmem_limit_bytes=64 * 1024 * 1024
        ),
    )(*operands)
    return restored.T[:, None, :]


def solution(mesh):
    placed = (
        P(("groups", "frame"), "row", "col"),
        P("row", "col"),
        P("row", "col"),
        P("row", "col"),
        P(),
        P(),
        P(("groups", "frame"), "row", "col", None),
        P(),
        P(),
        P("row", "col"),
        P(),
        P(),
    )
    sizes = (mesh.shape["frame"], mesh.shape["row"], mesh.shape["col"])
    return jax.shard_map(
        functools.partial(per_device, sizes),
        mesh=mesh,
        in_specs=placed,
        out_specs=P(("groups", "row"), "col", "frame"),
        check_vma=False,
    )
```

```python
import functools
import math

import jax
import jax.numpy as jnp
import ml_dtypes
import numpy as np
from jax import lax
from jax.experimental import pallas as pl
from jax.experimental.pallas import tpu as pltpu
from jax.sharding import PartitionSpec as P

PATCH = 128
PUPIL = 64
STEP = 64
HALF = 32
RIM = 48
KEPT = 72
MESH = pl.DeviceIdType.MESH
AROUND = [(i, j) for i in (-1, 0, 1) for j in (-1, 0, 1) if (i, j) != (0, 0)]


def split_table(table):
    table = table.astype(np.float32)
    high = table.astype(ml_dtypes.bfloat16)
    return high, (table - high.astype(np.float32)).astype(ml_dtypes.bfloat16)


def tables():
    n = PATCH
    turn = np.outer(np.arange(n), np.arange(n)) % n * (2.0 * math.pi / n)
    cosine, sine = np.cos(turn), np.sin(turn)
    blend = np.sin(math.pi * (np.arange(n) + 0.5) / n) ** 2
    pupil_x = np.zeros((2, 2, PUPIL, 2, 2, n))
    for q in range(2):
        pupil_x[0, q, :, q, 0] = cosine[:PUPIL]
        pupil_x[0, q, :, q, 1] = -sine[:PUPIL]
        pupil_x[1, q, :, q, 0] = sine[:PUPIL]
        pupil_x[1, q, :, q, 1] = cosine[:PUPIL]
    order = np.array([2 * j + q for q in range(2) for j in range(PUPIL // 2)])
    c, s = cosine[:, order], sine[:, order]
    pupil_y = np.block([[c, s], [-s, c]])
    half = n // 2 + 1
    front = np.zeros((2 * KEPT, n))
    front[:half] = cosine[:half]
    front[KEPT : KEPT + half] = sine[:half]
    across = np.block([[cosine, -sine], [-sine, -cosine]])
    back_x = np.block([[cosine, sine], [-sine, cosine]]) * np.tile(blend, 2)[None, :]
    weight = np.where((np.arange(half) % (n // 2)) == 0, 1.0, 2.0) / (n * n)
    back_y = np.zeros((n, 2 * KEPT))
    back_y[:, :half] = cosine[:, :half] * weight * blend[:, None]
    back_y[:, KEPT : KEPT + half] = -sine[:, :half] * weight * blend[:, None]
    pupil_x = pupil_x.reshape(256, 2, 256)
    side = np.zeros((256, 256))
    side[:, :n] = pupil_y
    side[: 2 * KEPT, n:] = front
    last = np.zeros((n, 256))
    last[:, : 2 * KEPT] = back_y
    whole = [pupil_x[:, 0], pupil_x[:, 1], across, back_x, side, last]
    return np.stack(split_table(np.concatenate(whole, axis=0)))


def halves(value):
    high = value.astype(jnp.bfloat16)
    return high, (value - high.astype(jnp.float32)).astype(jnp.bfloat16)


def dot(left, right):
    return jnp.dot(left, right, preferred_element_type=jnp.float32)


def dot3(left, right):
    return dot(left[0], right[0]) + (dot(left[1], right[0]) + dot(left[0], right[1]))


def cos_sin(angle):
    quarter = jnp.floor(angle * (2.0 / math.pi) + 0.5)
    rest = (angle - quarter * 1.5703125) - quarter * (math.pi / 2 - 1.5703125)
    sq = rest * rest
    s = rest + rest * sq * (-1 / 6 + sq * (1 / 120 + sq * (-1 / 5040 + sq * (1 / 362880))))
    c = 1.0 + sq * (-0.5 + sq * (1 / 24 + sq * (-1 / 720 + sq * (1 / 40320))))
    turn = quarter.astype(jnp.int32) & 3
    odd = (turn & 1) == 1
    cos_value, sin_value = jnp.where(odd, s, c), jnp.where(odd, c, s)
    return (
        jnp.where((turn == 1) | (turn == 2), -cos_value, cos_value),
        jnp.where(turn >= 2, -sin_value, sin_value),
    )


def band(taps, shape, lag):
    matrix = jnp.zeros(shape, jnp.float32)
    for t in range(taps.shape[0]):
        matrix = jnp.where(lag == t, taps[t], matrix)
    return halves(matrix)


def kernel(
    sizes,
    *refs,
):
    given, refs = refs[:13], refs[13:]
    out, held, refs = refs[0], refs[1:14], refs[14:]
    (raw, dark, gain, bad, taps_col, taps_row, levels, level_table, basis, apod, window_table, noise,
     table) = held
    (ext, coeff, coeff_all, phase_s, stage, strips, strip_s, pack, rims,
     a_send, a_recv, q_send, q_recv, b_send, b_recv, c_send, c_recv, in_sem) = refs
    frames, rows, cols = sizes
    g, me = lax.axis_index("groups"), lax.axis_index("frame")
    r, c = lax.axis_index("row"), lax.axis_index("col")
    tile_rows, tile_cols = dark.shape
    h = c * frames + me

    def inside(i, size):
        return (i >= 0) & (i < size)

    def tile_ok(dr, dc):
        return inside(r + dr, rows) & inside(c + dc, cols)

    def strip_ok(dr, dh):
        return inside(r + dr, rows) & inside(h + dh, cols * frames)

    def strip_device(dr, dh):
        to = h + dh
        return (g, to % frames, r + dr, to // frames)

    def peer(step):
        if frames & (frames - 1):
            return (me + step) % frames
        value, bit = me, 1
        while bit <= step:
            if step & bit:
                value = value + bit * (1 - 2 * ((value // bit) % 2))
            bit *= 2
        return value

    fetches = [pltpu.make_async_copy(given[i], held[i], in_sem.at[i]) for i in range(13)]
    for i in (0, 1, 2, 3, 6, 7, 4, 5, 12, 8, 9, 10, 11):
        fetches[i].start()

    barrier = pltpu.get_barrier_semaphore()
    expected = jnp.int32(frames - 1)
    for step in range(1, frames):
        pl.semaphore_signal(barrier, inc=1, device_id=(g, peer(step), r, c), device_id_type=MESH)
    for dr, dc in AROUND:
        ok = tile_ok(dr, dc)
        expected = expected + ok.astype(jnp.int32)

        @pl.when(ok)
        def _(dr=dr, dc=dc):
            pl.semaphore_signal(
                barrier, inc=1, device_id=(g, me, r + dr, c + dc), device_id_type=MESH
            )

        if dc:
            ok = strip_ok(dr, dc)
            expected = expected + ok.astype(jnp.int32)

            @pl.when(ok)
            def _(dr=dr, dc=dc):
                pl.semaphore_signal(
                    barrier, inc=1, device_id=strip_device(dr, dc), device_id_type=MESH
                )

    for i in range(4):
        fetches[i].wait()
    flat0 = (raw[0] - dark[...]) * gain[...]
    mean = 0.5 * (pltpu.roll(flat0, 1, 1) + pltpu.roll(flat0, tile_cols - 1, 1))
    ext[RIM : RIM + tile_rows, PATCH : PATCH + tile_cols] = jnp.where(bad[...] == 1, mean, flat0)
    fetches[6].wait()
    fetches[7].wait()
    ids = levels[...]
    picked = jnp.zeros(ids.shape, jnp.float32)
    for v in range(level_table.shape[0]):
        picked = jnp.where(ids == v, level_table[v], picked)
    modes = ids.shape[1]
    coeff[...] = jnp.zeros(coeff.shape, jnp.float32)
    coeff[:, :modes] = picked
    coeff_all[me] = coeff[...]

    row_src = {0: pl.ds(RIM, tile_rows), 1: pl.ds(tile_rows, RIM), -1: pl.ds(RIM, RIM)}
    row_dst = {0: pl.ds(RIM, tile_rows), 1: pl.ds(0, RIM), -1: pl.ds(RIM + tile_rows, RIM)}
    col_src = {0: pl.ds(PATCH, tile_cols), 1: pl.ds(tile_cols, PATCH), -1: pl.ds(PATCH, PATCH)}
    col_dst = {0: pl.ds(PATCH, tile_cols), 1: pl.ds(0, PATCH), -1: pl.ds(PATCH + tile_cols, PATCH)}

    def a_copy(i):
        dr, dc = AROUND[i]
        return pltpu.make_async_remote_copy(
            src_ref=ext.at[row_src[dr], col_src[dc]],
            dst_ref=ext.at[row_dst[dr], col_dst[dc]],
            send_sem=a_send.at[i],
            recv_sem=a_recv.at[i],
            device_id=(g, me, r + dr, c + dc),
            device_id_type=MESH,
        )

    def q_copy(step, source):
        return pltpu.make_async_remote_copy(
            src_ref=coeff,
            dst_ref=coeff_all.at[source],
            send_sem=q_send.at[step],
            recv_sem=q_recv.at[source],
            device_id=(g, peer(step), r, c),
            device_id_type=MESH,
        )

    height = strips.shape[1]
    if rows == 2:
        spans = [
            pl.ds(RIM, height - 2 * RIM),
            pl.ds(pl.multiple_of((height - RIM) * (1 - r), 16), RIM),
            pl.ds(pl.multiple_of(HALF + (height - RIM - HALF) * r, 16), RIM - HALF),
        ]
    else:
        spans = [pl.ds(RIM, height - 2 * RIM), pl.ds(0, RIM), pl.ds(height - RIM, RIM)]

    def b_copy(k, source, n):
        return pltpu.make_async_remote_copy(
            src_ref=stage.at[k, spans[n]],
            dst_ref=strips.at[source, spans[n]],
            send_sem=b_send.at[n, k],
            recv_sem=b_recv.at[n, source],
            device_id=(g, k, r, c),
            device_id_type=MESH,
        )

    def c_copy(i):
        dr, dh = AROUND[i]
        source = {
            0: pack.at[(dh + 1) // 2],
            -1: strip_s.at[pl.ds(0, HALF)],
            1: strip_s.at[pl.ds(height - HALF, HALF)],
        }[dr]
        return pltpu.make_async_remote_copy(
            src_ref=source,
            dst_ref=rims.at[i],
            send_sem=c_send.at[i],
            recv_sem=c_recv.at[i],
            device_id=strip_device(dr, dh),
            device_id_type=MESH,
        )

    lag = lax.broadcasted_iota(jnp.int32, (256, PATCH), 0) - lax.broadcasted_iota(
        jnp.int32, (256, PATCH), 1
    )
    fetches[4].wait()
    fetches[5].wait()
    col_bands = [band(taps_col, lag.shape, lag - first) for first in (81, 17)]
    shape = (height - 2 * RIM, tile_rows)
    lag = lax.broadcasted_iota(jnp.int32, shape, 1) - lax.broadcasted_iota(jnp.int32, shape, 0)
    row_band = band(taps_row, shape, lag - 1)
    pl.semaphore_wait(barrier, expected)
    for i, (dr, dc) in enumerate(AROUND):

        @pl.when(tile_ok(dr, dc))
        def _(i=i):
            a_copy(i).start()

    for step in range(1, frames):
        q_copy(step, me).start()

    for i, (dr, dc) in enumerate(AROUND):

        @pl.when(jnp.logical_not(tile_ok(-dr, -dc)))
        def _(dr=dr, dc=dc):
            y, x = row_dst[dr], col_dst[dc]
            ext[y, x] = jnp.zeros((y.size, x.size), jnp.float32)

        @pl.when(jnp.logical_not(strip_ok(-dr, -dc)))
        def _(i=i):
            rims[i] = jnp.zeros(rims.shape[1:], jnp.float32)

    def await_tiles(chosen):
        for i, (dr, dc) in enumerate(AROUND):
            if chosen(dr):

                @pl.when(tile_ok(-dr, -dc))
                def _(i=i):
                    a_copy(i).wait_recv()

    def shine(first, size, reach, low, high):
        band_part = [half[:size, :reach] for half in row_band]
        return halves(dot3(band_part, halves(ext[first : first + reach, low:high])))

    def correct(first, size, light, low, chosen):
        y_here = lax.broadcasted_iota(jnp.int32, (size, PATCH), 0) + (r * tile_rows - HALF + first)
        x_here = lax.broadcasted_iota(jnp.int32, (size, PATCH), 1) + (c * tile_cols - HALF)
        for k in chosen:
            begin = (STEP * k + 81) // PATCH * PATCH
            part = slice(begin - low, begin - low + 256)
            stray = dot3([half[:, part] for half in light], col_bands[k % 2])
            at = STEP * k + 96 - begin
            wide = ext[first + 16 : first + 16 + size, begin : begin + 256]
            here = pltpu.roll(wide, 256 - at, 1)[:, :PATCH]
            keep = inside(y_here, rows * tile_rows) & inside(x_here + STEP * k, cols * tile_cols)
            stage[k, first : first + size, :] = jnp.where(keep, here - stray, 0.0)

    def send_spans(chosen, windows):
        for k in windows:

            @pl.when(k != me)
            def _(k=k):
                for n in chosen:
                    b_copy(k, me, n).start()

    right_edge = PATCH + tile_cols
    inner = list(range(1, frames - 1))
    outer = [0, frames - 1]
    middle = shine(RIM, height - 2 * RIM, tile_rows, PATCH, right_edge)
    correct(RIM, height - 2 * RIM, middle, PATCH, inner)
    send_spans((0,), inner)
    await_tiles(lambda dr: dr == 0)
    left = shine(RIM, height - 2 * RIM, tile_rows, 0, PATCH)
    right = shine(RIM, height - 2 * RIM, tile_rows, right_edge, right_edge + PATCH)
    light = [jnp.concatenate(parts, axis=1) for parts in zip(left, middle, right)]
    correct(RIM, height - 2 * RIM, light, 0, outer)
    send_spans((0,), outer)
    await_tiles(lambda dr: dr != 0)
    for first in (0, height - RIM):
        light = shine(first, RIM, RIM + HALF, 0, right_edge + PATCH)
        correct(first, RIM, light, 0, range(frames))
    send_spans((1, 2), range(frames))
    strips[me] = stage[me]
    if rows == 2:
        edge = pl.ds(pl.multiple_of((height - HALF) * r, HALF), HALF)
        for step in range(1, frames):
            strips[peer(step), edge, :] = jnp.zeros((HALF, PATCH), jnp.float32)

    for i in (12, 8, 9, 10, 11):
        fetches[i].wait()
    y_at = lax.broadcasted_iota(jnp.int32, (PATCH, PATCH), 0)
    x_at = lax.broadcasted_iota(jnp.int32, (PATCH, PATCH), 1)
    flip = ((y_at + x_at) % PATCH == 0).astype(jnp.float32).astype(jnp.bfloat16)
    n_high, n_low = halves(noise[...])
    turned = dot(flip, n_high), dot(flip, n_low)
    turned = dot(turned[0].astype(jnp.bfloat16), flip) + dot(turned[1].astype(jnp.bfloat16), flip)
    noises = (noise[:KEPT, :], turned[:KEPT, :])
    weights = []
    for a in range(2):
        chosen = apod[a, me]
        line = jnp.zeros((1, PATCH), jnp.float32)
        for v in range(window_table.shape[0]):
            line = jnp.where(chosen == v, window_table[v : v + 1, :], line)
        column = jnp.sum(jnp.where(y_at == x_at, line, 0.0), axis=1, keepdims=True)
        weights.append(column * line)
    basis_parts = halves(basis[...])

    px = [tuple(table[i, 256 * q : 256 * q + 256, :] for i in range(2)) for q in range(2)]
    ac = tuple(table[i, 512:768, :] for i in range(2))
    bx = tuple(table[i, 768:1024, :] for i in range(2))
    py = tuple(table[i, 1024:1280, :PATCH] for i in range(2))
    fr = tuple(table[i, 1024 : 1024 + 2 * KEPT, PATCH:] for i in range(2))
    by = tuple(table[i, 1280 : 1280 + PATCH, : 2 * KEPT] for i in range(2))
    for step in range(1, frames):
        q_copy(step, peer(step)).wait_recv()
    count = 2 * frames
    mine = [
        coeff_all[peer(step), pl.ds(a * frames + me, 1), :]
        for step in range(frames)
        for a in range(2)
    ]
    phase = dot3(halves(jnp.concatenate(mine, axis=0)[:, :modes]), basis_parts)
    lines = PUPIL // 2
    for j in range(lines):
        phase_s[pl.ds(j, count, stride=lines), :] = phase[:, j * PATCH : (j + 1) * PATCH]
    y2 = 2 * (2 * y_at[:lines] + x_at[:lines] // PUPIL) - (PUPIL - 1)
    x2 = 2 * (x_at[:lines] % PUPIL) - (PUPIL - 1)
    stop = (y2 * y2 + x2 * x2 <= PUPIL * PUPIL).astype(jnp.float32)
    stop = jnp.concatenate([stop] * count, axis=0)
    real, imag = cos_sin(phase_s[...])
    field = jnp.concatenate([real * stop, imag * stop], axis=1)
    field = halves(field)
    field = [dot3(field, px[q]) for q in range(2)]
    picks = []
    for p in range(count):
        part = [field[q][p * lines : (p + 1) * lines] for q in range(2)]
        picks.append(
            jnp.concatenate(
                [part[0][:, :PATCH], part[1][:, :PATCH], part[0][:, PATCH:], part[1][:, PATCH:]],
                axis=0,
            )
        )

    def spectrum(images):
        first = dot3(fr, halves(jnp.concatenate(images, axis=1)))
        parts = [
            jnp.concatenate(
                [
                    first[:KEPT, i * PATCH : (i + 1) * PATCH],
                    first[KEPT:, i * PATCH : (i + 1) * PATCH],
                ],
                axis=1,
            )
            for i in range(len(images))
        ]
        return dot3(halves(jnp.concatenate(parts, axis=0)), ac)

    optics = []
    for step in range(frames):
        pair = jnp.concatenate(picks[2 * step : 2 * step + 2], axis=1)
        spread = dot3(py, halves(pair))
        power = spread[:PATCH] * spread[:PATCH] + spread[PATCH:] * spread[PATCH:]
        images = []
        for a in range(2):
            one = power[:, a * PATCH : (a + 1) * PATCH]
            images.append(one * (1.0 / jnp.sum(one, axis=(0, 1), keepdims=True)))
        optics.append(spectrum(images))

    totals = [[jnp.zeros((KEPT, PATCH), jnp.float32)] * 3 for a in range(2)]
    for step in range(frames):
        if step:
            for n in range(3):
                b_copy(peer(step), peer(step), n).wait_recv()
        images = [
            strips[peer(step), a * STEP : a * STEP + PATCH, :] * weights[a] for a in range(2)
        ]
        image = spectrum(images)
        for a in range(2):
            lot = slice(a * KEPT, (a + 1) * KEPT)
            i_re, i_im = image[lot, :PATCH], image[lot, PATCH:]
            o_re, o_im = optics[step][lot, :PATCH], optics[step][lot, PATCH:]
            total = totals[a]
            totals[a] = [
                total[0] + o_re * i_re + o_im * i_im,
                total[1] + o_re * i_im - o_im * i_re,
                total[2] + o_re * o_re + o_im * o_im,
            ]

    whole = []
    for a in range(2):
        num_re, num_im, power = totals[a]
        factor = 0.5 / (power + noises[0]) + 0.5 / (power + noises[1])
        whole.append(jnp.concatenate([num_re * factor, num_im * factor], axis=1))
    turned = dot3(halves(jnp.concatenate(whole, axis=0)), bx)
    sides = [
        jnp.concatenate(
            [turned[a * KEPT : (a + 1) * KEPT, :PATCH], turned[a * KEPT : (a + 1) * KEPT, PATCH:]],
            axis=0,
        )
        for a in range(2)
    ]
    contrib = dot3(by, halves(jnp.concatenate(sides, axis=1)))
    upper, lower = contrib[:, :PATCH], contrib[:, PATCH:]
    strip = jnp.concatenate([upper[:STEP], upper[STEP:] + lower[:STEP], lower[STEP:]], axis=0)
    strip_s[...] = strip
    body = strip[HALF : HALF + tile_rows]
    lane = lax.broadcasted_iota(jnp.int32, (HALF, PATCH), 1)
    for side in range(2):
        packed = jnp.zeros((HALF, PATCH), jnp.float32)
        for q in range(4):
            shift = (HALF * q + HALF * side) % PATCH
            rolled = body[q * HALF : (q + 1) * HALF]
            if shift:
                rolled = pltpu.roll(rolled, shift, 1)
            packed = jnp.where(lane // HALF == q, rolled, packed)
        pack[side] = packed
    for i, (dr, dh) in enumerate(AROUND):

        @pl.when(strip_ok(dr, dh))
        def _(i=i):
            c_copy(i).start()

    for i, (dr, dc) in enumerate(AROUND):

        @pl.when(tile_ok(dr, dc))
        def _(i=i):
            a_copy(i).wait_send()

    for step in range(1, frames):
        q_copy(step, me).wait_send()
        for n in range(3):
            b_copy(peer(step), me, n).wait_send()

    for i, (dr, dh) in enumerate(AROUND):

        @pl.when(strip_ok(-dr, -dh))
        def _(i=i):
            c_copy(i).wait_recv()

    from_left, from_right = lane // HALF == 1, lane // HALF == 2
    blocks = []
    for q in range(4):
        value = body[q * HALF : (q + 1) * HALF]
        for i, (dr, dh) in enumerate(AROUND):
            if dr == 0:
                goal = 1 if dh == 1 else 2
                shift = (HALF * (goal - q)) % PATCH
                got = pltpu.roll(rims[i], shift, 1) if shift else rims[i]
                value = value + jnp.where(from_left if dh == 1 else from_right, got, 0.0)
            elif (dr == 1 and q == 0) or (dr == -1 and q == 3):
                if dh == 0:
                    value = value + rims[i]
                else:
                    got = pltpu.roll(rims[i], STEP, 1)
                    value = value + jnp.where(from_left if dh == 1 else from_right, got, 0.0)
        blocks.append(value)
    out[...] = jnp.concatenate(blocks, axis=0).T[HALF : HALF + STEP, :]

    for i, (dr, dh) in enumerate(AROUND):

        @pl.when(strip_ok(dr, dh))
        def _(i=i):
            c_copy(i).wait_send()


def per_device(
    sizes,
    raw, dark, gain, bad, taps_col, taps_row, levels, level_table, basis, apod_index, window_table, noise,
):
    frames = sizes[0]
    tile_rows, tile_cols = dark.shape
    height = tile_rows + STEP
    count = 2 * frames
    vmem = pl.BlockSpec(memory_space=pltpu.VMEM)
    operands = [
        raw, dark, gain, bad, taps_col, taps_row,
        levels.reshape(count, levels.shape[3]),
        level_table, basis, apod_index, window_table, noise,
        jnp.asarray(tables()),
    ]
    held = [
        (pltpu.SMEM if i in (4, 5, 7, 9) else pltpu.VMEM)(operand.shape, operand.dtype)
        for i, operand in enumerate(operands)
    ]
    dma = pltpu.SemaphoreType.DMA
    restored = pl.pallas_call(
        functools.partial(kernel, sizes),
        out_shape=jax.ShapeDtypeStruct((STEP, tile_rows), jnp.float32),
        in_specs=[pl.BlockSpec(memory_space=pltpu.HBM)] * 13,
        out_specs=vmem,
        scratch_shapes=held
        + [
            pltpu.VMEM((tile_rows + 2 * RIM, tile_cols + 2 * PATCH), jnp.float32),
            pltpu.VMEM((count, PATCH), jnp.float32),
            pltpu.VMEM((frames, count, PATCH), jnp.float32),
            pltpu.VMEM((count * PUPIL // 2, PATCH), jnp.float32),
            pltpu.VMEM((frames, height, PATCH), jnp.float32),
            pltpu.VMEM((frames, height, PATCH), jnp.float32),
            pltpu.VMEM((height, PATCH), jnp.float32),
            pltpu.VMEM((2, HALF, PATCH), jnp.float32),
            pltpu.VMEM((8, HALF, PATCH), jnp.float32),
            dma((8,)),
            dma((8,)),
            dma((frames,)),
            dma((frames,)),
            dma((3, frames)),
            dma((3, frames)),
            dma((8,)),
            dma((8,)),
            dma((13,)),
        ],
        compiler_params=pltpu.CompilerParams(
            collective_id=0, has_side_effects=True, vmem_limit_bytes=64 * 1024 * 1024
        ),
    )(*operands)
    return restored.T[:, None, :]


def solution(mesh):
    placed = (
        P(("groups", "frame"), "row", "col"),
        P("row", "col"),
        P("row", "col"),
        P("row", "col"),
        P(),
        P(),
        P(("groups", "frame"), "row", "col", None),
        P(),
        P(),
        P("row", "col"),
        P(),
        P(),
    )
    sizes = (mesh.shape["frame"], mesh.shape["row"], mesh.shape["col"])
    return jax.shard_map(
        functools.partial(per_device, sizes),
        mesh=mesh,
        in_specs=placed,
        out_specs=P(("groups", "row"), "col", "frame"),
        check_vma=False,
    )
```

```python
import functools
import math

import jax
import jax.numpy as jnp
import ml_dtypes
import numpy as np
from jax import lax
from jax.experimental import pallas as pl
from jax.experimental.pallas import tpu as pltpu
from jax.sharding import PartitionSpec as P

PATCH = 128
PUPIL = 64
STEP = 64
HALF = 32
RIM = 48
KEPT = 72
MESH = pl.DeviceIdType.MESH
AROUND = [(i, j) for i in (-1, 0, 1) for j in (-1, 0, 1) if (i, j) != (0, 0)]


def split_table(table):
    table = table.astype(np.float32)
    high = table.astype(ml_dtypes.bfloat16)
    return high, (table - high.astype(np.float32)).astype(ml_dtypes.bfloat16)


def tables():
    n = PATCH
    turn = np.outer(np.arange(n), np.arange(n)) % n * (2.0 * math.pi / n)
    cosine, sine = np.cos(turn), np.sin(turn)
    blend = np.sin(math.pi * (np.arange(n) + 0.5) / n) ** 2
    pupil_x = np.zeros((2, 2, PUPIL, 2, 2, n))
    for q in range(2):
        pupil_x[0, q, :, q, 0] = cosine[:PUPIL]
        pupil_x[0, q, :, q, 1] = -sine[:PUPIL]
        pupil_x[1, q, :, q, 0] = sine[:PUPIL]
        pupil_x[1, q, :, q, 1] = cosine[:PUPIL]
    order = np.array([2 * j + q for q in range(2) for j in range(PUPIL // 2)])
    c, s = cosine[:, order], sine[:, order]
    pupil_y = np.block([[c, s], [-s, c]])
    half = n // 2 + 1
    front = np.zeros((2 * KEPT, n))
    front[:half] = cosine[:half]
    front[KEPT : KEPT + half] = sine[:half]
    across = np.block([[cosine, -sine], [-sine, -cosine]])
    back_x = np.block([[cosine, sine], [-sine, cosine]]) * np.tile(blend, 2)[None, :]
    weight = np.where((np.arange(half) % (n // 2)) == 0, 1.0, 2.0) / (n * n)
    back_y = np.zeros((n, 2 * KEPT))
    back_y[:, :half] = cosine[:, :half] * weight * blend[:, None]
    back_y[:, KEPT : KEPT + half] = -sine[:, :half] * weight * blend[:, None]
    pupil_x = pupil_x.reshape(256, 2, 256)
    side = np.zeros((256, 256))
    side[:, :n] = pupil_y
    side[: 2 * KEPT, n:] = front
    last = np.zeros((n, 256))
    last[:, : 2 * KEPT] = back_y
    whole = [pupil_x[:, 0], pupil_x[:, 1], across, back_x, side, last]
    return np.stack(split_table(np.concatenate(whole, axis=0)))


def halves(value):
    high = value.astype(jnp.bfloat16)
    return high, (value - high.astype(jnp.float32)).astype(jnp.bfloat16)


def dot(left, right):
    return jnp.dot(left, right, preferred_element_type=jnp.float32)


def dot3(left, right):
    return dot(left[0], right[0]) + (dot(left[1], right[0]) + dot(left[0], right[1]))


def cos_sin(angle):
    quarter = jnp.floor(angle * (2.0 / math.pi) + 0.5)
    rest = (angle - quarter * 1.5703125) - quarter * (math.pi / 2 - 1.5703125)
    sq = rest * rest
    s = rest + rest * sq * (-1 / 6 + sq * (1 / 120 + sq * (-1 / 5040 + sq * (1 / 362880))))
    c = 1.0 + sq * (-0.5 + sq * (1 / 24 + sq * (-1 / 720 + sq * (1 / 40320))))
    turn = quarter.astype(jnp.int32) & 3
    odd = (turn & 1) == 1
    cos_value, sin_value = jnp.where(odd, s, c), jnp.where(odd, c, s)
    return (
        jnp.where((turn == 1) | (turn == 2), -cos_value, cos_value),
        jnp.where(turn >= 2, -sin_value, sin_value),
    )


def band(taps, shape, lag):
    matrix = jnp.zeros(shape, jnp.float32)
    for t in range(taps.shape[0]):
        matrix = jnp.where(lag == t, taps[t], matrix)
    return halves(matrix)


def kernel(
    sizes,
    *refs,
):
    given, refs = refs[:13], refs[13:]
    out, held, refs = refs[0], refs[1:14], refs[14:]
    (raw, dark, gain, bad, taps_col, taps_row, levels, level_table, basis, apod, window_table, noise,
     table) = held
    (ext, coeff, coeff_all, phase_s, stage, strips, strip_s, pack, rims,
     a_send, a_recv, q_send, q_recv, b_send, b_recv, c_send, c_recv, in_sem) = refs
    frames, rows, cols = sizes
    g, me = lax.axis_index("groups"), lax.axis_index("frame")
    r, c = lax.axis_index("row"), lax.axis_index("col")
    tile_rows, tile_cols = dark.shape
    h = c * frames + me

    def inside(i, size):
        return (i >= 0) & (i < size)

    def tile_ok(dr, dc):
        return inside(r + dr, rows) & inside(c + dc, cols)

    def strip_ok(dr, dh):
        return inside(r + dr, rows) & inside(h + dh, cols * frames)

    def strip_device(dr, dh):
        to = h + dh
        return (g, to % frames, r + dr, to // frames)

    def peer(step):
        if frames & (frames - 1):
            return (me + step) % frames
        value, bit = me, 1
        while bit <= step:
            if step & bit:
                value = value + bit * (1 - 2 * ((value // bit) % 2))
            bit *= 2
        return value

    fetches = [pltpu.make_async_copy(given[i], held[i], in_sem.at[i]) for i in range(13)]
    for i in (0, 1, 2, 3, 6, 7, 4, 5, 12, 8, 9, 10, 11):
        fetches[i].start()

    barrier = pltpu.get_barrier_semaphore()
    expected = jnp.int32(frames - 1)
    for step in range(1, frames):
        pl.semaphore_signal(barrier, inc=1, device_id=(g, peer(step), r, c), device_id_type=MESH)
    for dr, dc in AROUND:
        ok = tile_ok(dr, dc)
        expected = expected + ok.astype(jnp.int32)

        @pl.when(ok)
        def _(dr=dr, dc=dc):
            pl.semaphore_signal(
                barrier, inc=1, device_id=(g, me, r + dr, c + dc), device_id_type=MESH
            )

        if dc:
            ok = strip_ok(dr, dc)
            expected = expected + ok.astype(jnp.int32)

            @pl.when(ok)
            def _(dr=dr, dc=dc):
                pl.semaphore_signal(
                    barrier, inc=1, device_id=strip_device(dr, dc), device_id_type=MESH
                )

    for i in range(4):
        fetches[i].wait()
    flat0 = (raw[0] - dark[...]) * gain[...]
    mean = 0.5 * (pltpu.roll(flat0, 1, 1) + pltpu.roll(flat0, tile_cols - 1, 1))
    ext[RIM : RIM + tile_rows, PATCH : PATCH + tile_cols] = jnp.where(bad[...] == 1, mean, flat0)
    fetches[6].wait()
    fetches[7].wait()
    ids = levels[...]
    picked = jnp.zeros(ids.shape, jnp.float32)
    for v in range(level_table.shape[0]):
        picked = jnp.where(ids == v, level_table[v], picked)
    modes = ids.shape[1]
    coeff[...] = jnp.zeros(coeff.shape, jnp.float32)
    coeff[:, :modes] = picked
    coeff_all[me] = coeff[...]

    row_src = {0: pl.ds(RIM, tile_rows), 1: pl.ds(tile_rows, RIM), -1: pl.ds(RIM, RIM)}
    row_dst = {0: pl.ds(RIM, tile_rows), 1: pl.ds(0, RIM), -1: pl.ds(RIM + tile_rows, RIM)}
    col_src = {0: pl.ds(PATCH, tile_cols), 1: pl.ds(tile_cols, PATCH), -1: pl.ds(PATCH, PATCH)}
    col_dst = {0: pl.ds(PATCH, tile_cols), 1: pl.ds(0, PATCH), -1: pl.ds(PATCH + tile_cols, PATCH)}

    def a_copy(i):
        dr, dc = AROUND[i]
        return pltpu.make_async_remote_copy(
            src_ref=ext.at[row_src[dr], col_src[dc]],
            dst_ref=ext.at[row_dst[dr], col_dst[dc]],
            send_sem=a_send.at[i],
            recv_sem=a_recv.at[i],
            device_id=(g, me, r + dr, c + dc),
            device_id_type=MESH,
        )

    def q_copy(step, source):
        return pltpu.make_async_remote_copy(
            src_ref=coeff,
            dst_ref=coeff_all.at[source],
            send_sem=q_send.at[step],
            recv_sem=q_recv.at[source],
            device_id=(g, peer(step), r, c),
            device_id_type=MESH,
        )

    height = strips.shape[1]
    if rows == 2:
        spans = [
            pl.ds(RIM, height - 2 * RIM),
            pl.ds(pl.multiple_of((height - RIM) * (1 - r), 16), RIM),
            pl.ds(pl.multiple_of(HALF + (height - RIM - HALF) * r, 16), RIM - HALF),
        ]
    else:
        spans = [pl.ds(RIM, height - 2 * RIM), pl.ds(0, RIM), pl.ds(height - RIM, RIM)]

    def b_copy(k, source, n):
        return pltpu.make_async_remote_copy(
            src_ref=stage.at[k, spans[n]],
            dst_ref=strips.at[source, spans[n]],
            send_sem=b_send.at[n, k],
            recv_sem=b_recv.at[n, source],
            device_id=(g, k, r, c),
            device_id_type=MESH,
        )

    def c_copy(i):
        dr, dh = AROUND[i]
        source = {
            0: pack.at[(dh + 1) // 2],
            -1: strip_s.at[pl.ds(0, HALF)],
            1: strip_s.at[pl.ds(height - HALF, HALF)],
        }[dr]
        return pltpu.make_async_remote_copy(
            src_ref=source,
            dst_ref=rims.at[i],
            send_sem=c_send.at[i],
            recv_sem=c_recv.at[i],
            device_id=strip_device(dr, dh),
            device_id_type=MESH,
        )

    lag = lax.broadcasted_iota(jnp.int32, (256, PATCH), 0) - lax.broadcasted_iota(
        jnp.int32, (256, PATCH), 1
    )
    fetches[4].wait()
    fetches[5].wait()
    col_bands = [band(taps_col, lag.shape, lag - first) for first in (81, 17)]
    shape = (height - 2 * RIM, tile_rows)
    lag = lax.broadcasted_iota(jnp.int32, shape, 1) - lax.broadcasted_iota(jnp.int32, shape, 0)
    row_band = band(taps_row, shape, lag - 1)
    pl.semaphore_wait(barrier, expected)
    for i, (dr, dc) in enumerate(AROUND):

        @pl.when(tile_ok(dr, dc))
        def _(i=i):
            a_copy(i).start()

    for step in range(1, frames):
        q_copy(step, me).start()

    for i, (dr, dc) in enumerate(AROUND):

        @pl.when(jnp.logical_not(tile_ok(-dr, -dc)))
        def _(dr=dr, dc=dc):
            y, x = row_dst[dr], col_dst[dc]
            ext[y, x] = jnp.zeros((y.size, x.size), jnp.float32)

        @pl.when(jnp.logical_not(strip_ok(-dr, -dc)))
        def _(i=i):
            rims[i] = jnp.zeros(rims.shape[1:], jnp.float32)

    def await_tiles(chosen):
        for i, (dr, dc) in enumerate(AROUND):
            if chosen(dr):

                @pl.when(tile_ok(-dr, -dc))
                def _(i=i):
                    a_copy(i).wait_recv()

    def shine(first, size, reach, low, high):
        band_part = [half[:size, :reach] for half in row_band]
        return halves(dot3(band_part, halves(ext[first : first + reach, low:high])))

    def correct(first, size, light, low, chosen):
        y_here = lax.broadcasted_iota(jnp.int32, (size, PATCH), 0) + (r * tile_rows - HALF + first)
        x_here = lax.broadcasted_iota(jnp.int32, (size, PATCH), 1) + (c * tile_cols - HALF)
        for k in chosen:
            begin = (STEP * k + 81) // PATCH * PATCH
            part = slice(begin - low, begin - low + 256)
            stray = dot3([half[:, part] for half in light], col_bands[k % 2])
            at = STEP * k + 96 - begin
            wide = ext[first + 16 : first + 16 + size, begin : begin + 256]
            here = pltpu.roll(wide, 256 - at, 1)[:, :PATCH]
            keep = inside(y_here, rows * tile_rows) & inside(x_here + STEP * k, cols * tile_cols)
            stage[k, first : first + size, :] = jnp.where(keep, here - stray, 0.0)

    def send_spans(chosen, windows):
        for k in windows:

            @pl.when(k != me)
            def _(k=k):
                for n in chosen:
                    b_copy(k, me, n).start()

    right_edge = PATCH + tile_cols
    inner = list(range(1, frames - 1))
    outer = [0, frames - 1]
    middle = shine(RIM, height - 2 * RIM, tile_rows, PATCH, right_edge)
    correct(RIM, height - 2 * RIM, middle, PATCH, inner)
    send_spans((0,), inner)
    await_tiles(lambda dr: dr == 0)
    left = shine(RIM, height - 2 * RIM, tile_rows, 0, PATCH)
    right = shine(RIM, height - 2 * RIM, tile_rows, right_edge, right_edge + PATCH)
    light = [jnp.concatenate(parts, axis=1) for parts in zip(left, middle, right)]
    correct(RIM, height - 2 * RIM, light, 0, outer)
    send_spans((0,), outer)
    await_tiles(lambda dr: dr != 0)
    ends = (0, height - RIM)
    lights = [shine(first, RIM, RIM + HALF, 0, right_edge + PATCH) for first in ends]
    for k in range(frames):
        for first, light in zip(ends, lights):
            correct(first, RIM, light, 0, [k])
        send_spans((1, 2), [k])
    strips[me] = stage[me]
    if rows == 2:
        edge = pl.ds(pl.multiple_of((height - HALF) * r, HALF), HALF)
        for step in range(1, frames):
            strips[peer(step), edge, :] = jnp.zeros((HALF, PATCH), jnp.float32)

    for i in (12, 8, 9, 10, 11):
        fetches[i].wait()
    y_at = lax.broadcasted_iota(jnp.int32, (PATCH, PATCH), 0)
    x_at = lax.broadcasted_iota(jnp.int32, (PATCH, PATCH), 1)
    flip = ((y_at + x_at) % PATCH == 0).astype(jnp.float32).astype(jnp.bfloat16)
    n_high, n_low = halves(noise[...])
    turned = dot(flip, n_high), dot(flip, n_low)
    turned = dot(turned[0].astype(jnp.bfloat16), flip) + dot(turned[1].astype(jnp.bfloat16), flip)
    noises = (noise[:KEPT, :], turned[:KEPT, :])
    weights = []
    for a in range(2):
        chosen = apod[a, me]
        line = jnp.zeros((1, PATCH), jnp.float32)
        for v in range(window_table.shape[0]):
            line = jnp.where(chosen == v, window_table[v : v + 1, :], line)
        column = jnp.sum(jnp.where(y_at == x_at, line, 0.0), axis=1, keepdims=True)
        weights.append(column * line)
    basis_parts = halves(basis[...])

    px = [tuple(table[i, 256 * q : 256 * q + 256, :] for i in range(2)) for q in range(2)]
    ac = tuple(table[i, 512:768, :] for i in range(2))
    bx = tuple(table[i, 768:1024, :] for i in range(2))
    py = tuple(table[i, 1024:1280, :PATCH] for i in range(2))
    fr = tuple(table[i, 1024 : 1024 + 2 * KEPT, PATCH:] for i in range(2))
    by = tuple(table[i, 1280 : 1280 + PATCH, : 2 * KEPT] for i in range(2))
    for step in range(1, frames):
        q_copy(step, peer(step)).wait_recv()
    count = 2 * frames
    mine = [
        coeff_all[peer(step), pl.ds(a * frames + me, 1), :]
        for step in range(frames)
        for a in range(2)
    ]
    phase = dot3(halves(jnp.concatenate(mine, axis=0)[:, :modes]), basis_parts)
    lines = PUPIL // 2
    for j in range(lines):
        phase_s[pl.ds(j, count, stride=lines), :] = phase[:, j * PATCH : (j + 1) * PATCH]
    y2 = 2 * (2 * y_at[:lines] + x_at[:lines] // PUPIL) - (PUPIL - 1)
    x2 = 2 * (x_at[:lines] % PUPIL) - (PUPIL - 1)
    stop = (y2 * y2 + x2 * x2 <= PUPIL * PUPIL).astype(jnp.float32)
    stop = jnp.concatenate([stop] * count, axis=0)
    real, imag = cos_sin(phase_s[...])
    field = jnp.concatenate([real * stop, imag * stop], axis=1)
    field = halves(field)
    field = [dot3(field, px[q]) for q in range(2)]
    picks = []
    for p in range(count):
        part = [field[q][p * lines : (p + 1) * lines] for q in range(2)]
        picks.append(
            jnp.concatenate(
                [part[0][:, :PATCH], part[1][:, :PATCH], part[0][:, PATCH:], part[1][:, PATCH:]],
                axis=0,
            )
        )

    def spectrum(images):
        first = dot3(fr, halves(jnp.concatenate(images, axis=1)))
        parts = [
            jnp.concatenate(
                [
                    first[:KEPT, i * PATCH : (i + 1) * PATCH],
                    first[KEPT:, i * PATCH : (i + 1) * PATCH],
                ],
                axis=1,
            )
            for i in range(len(images))
        ]
        return dot3(halves(jnp.concatenate(parts, axis=0)), ac)

    optics = []
    for step in range(frames):
        pair = jnp.concatenate(picks[2 * step : 2 * step + 2], axis=1)
        spread = dot3(py, halves(pair))
        power = spread[:PATCH] * spread[:PATCH] + spread[PATCH:] * spread[PATCH:]
        images = []
        for a in range(2):
            one = power[:, a * PATCH : (a + 1) * PATCH]
            images.append(one * (1.0 / jnp.sum(one, axis=(0, 1), keepdims=True)))
        optics.append(spectrum(images))

    totals = [[jnp.zeros((KEPT, PATCH), jnp.float32)] * 3 for a in range(2)]
    for step in range(frames):
        if step:
            for n in range(3):
                b_copy(peer(step), peer(step), n).wait_recv()
        images = [
            strips[peer(step), a * STEP : a * STEP + PATCH, :] * weights[a] for a in range(2)
        ]
        image = spectrum(images)
        for a in range(2):
            lot = slice(a * KEPT, (a + 1) * KEPT)
            i_re, i_im = image[lot, :PATCH], image[lot, PATCH:]
            o_re, o_im = optics[step][lot, :PATCH], optics[step][lot, PATCH:]
            total = totals[a]
            totals[a] = [
                total[0] + o_re * i_re + o_im * i_im,
                total[1] + o_re * i_im - o_im * i_re,
                total[2] + o_re * o_re + o_im * o_im,
            ]

    whole = []
    for a in range(2):
        num_re, num_im, power = totals[a]
        factor = 0.5 / (power + noises[0]) + 0.5 / (power + noises[1])
        whole.append(jnp.concatenate([num_re * factor, num_im * factor], axis=1))
    turned = dot3(halves(jnp.concatenate(whole, axis=0)), bx)
    sides = [
        jnp.concatenate(
            [turned[a * KEPT : (a + 1) * KEPT, :PATCH], turned[a * KEPT : (a + 1) * KEPT, PATCH:]],
            axis=0,
        )
        for a in range(2)
    ]
    contrib = dot3(by, halves(jnp.concatenate(sides, axis=1)))
    upper, lower = contrib[:, :PATCH], contrib[:, PATCH:]
    strip = jnp.concatenate([upper[:STEP], upper[STEP:] + lower[:STEP], lower[STEP:]], axis=0)
    strip_s[...] = strip
    body = strip[HALF : HALF + tile_rows]
    lane = lax.broadcasted_iota(jnp.int32, (HALF, PATCH), 1)
    for side in range(2):
        packed = jnp.zeros((HALF, PATCH), jnp.float32)
        for q in range(4):
            shift = (HALF * q + HALF * side) % PATCH
            rolled = body[q * HALF : (q + 1) * HALF]
            if shift:
                rolled = pltpu.roll(rolled, shift, 1)
            packed = jnp.where(lane // HALF == q, rolled, packed)
        pack[side] = packed
    for i, (dr, dh) in enumerate(AROUND):

        @pl.when(strip_ok(dr, dh))
        def _(i=i):
            c_copy(i).start()

    for i, (dr, dc) in enumerate(AROUND):

        @pl.when(tile_ok(dr, dc))
        def _(i=i):
            a_copy(i).wait_send()

    for step in range(1, frames):
        q_copy(step, me).wait_send()
        for n in range(3):
            b_copy(peer(step), me, n).wait_send()

    for i, (dr, dh) in enumerate(AROUND):

        @pl.when(strip_ok(-dr, -dh))
        def _(i=i):
            c_copy(i).wait_recv()

    from_left, from_right = lane // HALF == 1, lane // HALF == 2
    blocks = []
    for q in range(4):
        value = body[q * HALF : (q + 1) * HALF]
        for i, (dr, dh) in enumerate(AROUND):
            if dr == 0:
                goal = 1 if dh == 1 else 2
                shift = (HALF * (goal - q)) % PATCH
                got = pltpu.roll(rims[i], shift, 1) if shift else rims[i]
                value = value + jnp.where(from_left if dh == 1 else from_right, got, 0.0)
            elif (dr == 1 and q == 0) or (dr == -1 and q == 3):
                if dh == 0:
                    value = value + rims[i]
                else:
                    got = pltpu.roll(rims[i], STEP, 1)
                    value = value + jnp.where(from_left if dh == 1 else from_right, got, 0.0)
        blocks.append(value)
    out[...] = jnp.concatenate(blocks, axis=0).T[HALF : HALF + STEP, :]

    for i, (dr, dh) in enumerate(AROUND):

        @pl.when(strip_ok(dr, dh))
        def _(i=i):
            c_copy(i).wait_send()


def per_device(
    sizes,
    raw, dark, gain, bad, taps_col, taps_row, levels, level_table, basis, apod_index, window_table, noise,
):
    frames = sizes[0]
    tile_rows, tile_cols = dark.shape
    height = tile_rows + STEP
    count = 2 * frames
    vmem = pl.BlockSpec(memory_space=pltpu.VMEM)
    operands = [
        raw, dark, gain, bad, taps_col, taps_row,
        levels.reshape(count, levels.shape[3]),
        level_table, basis, apod_index, window_table, noise,
        jnp.asarray(tables()),
    ]
    held = [
        (pltpu.SMEM if i in (4, 5, 7, 9) else pltpu.VMEM)(operand.shape, operand.dtype)
        for i, operand in enumerate(operands)
    ]
    dma = pltpu.SemaphoreType.DMA
    restored = pl.pallas_call(
        functools.partial(kernel, sizes),
        out_shape=jax.ShapeDtypeStruct((STEP, tile_rows), jnp.float32),
        in_specs=[pl.BlockSpec(memory_space=pltpu.HBM)] * 13,
        out_specs=vmem,
        scratch_shapes=held
        + [
            pltpu.VMEM((tile_rows + 2 * RIM, tile_cols + 2 * PATCH), jnp.float32),
            pltpu.VMEM((count, PATCH), jnp.float32),
            pltpu.VMEM((frames, count, PATCH), jnp.float32),
            pltpu.VMEM((count * PUPIL // 2, PATCH), jnp.float32),
            pltpu.VMEM((frames, height, PATCH), jnp.float32),
            pltpu.VMEM((frames, height, PATCH), jnp.float32),
            pltpu.VMEM((height, PATCH), jnp.float32),
            pltpu.VMEM((2, HALF, PATCH), jnp.float32),
            pltpu.VMEM((8, HALF, PATCH), jnp.float32),
            dma((8,)),
            dma((8,)),
            dma((frames,)),
            dma((frames,)),
            dma((3, frames)),
            dma((3, frames)),
            dma((8,)),
            dma((8,)),
            dma((13,)),
        ],
        compiler_params=pltpu.CompilerParams(
            collective_id=0, has_side_effects=True, vmem_limit_bytes=64 * 1024 * 1024
        ),
    )(*operands)
    return restored.T[:, None, :]


def solution(mesh):
    placed = (
        P(("groups", "frame"), "row", "col"),
        P("row", "col"),
        P("row", "col"),
        P("row", "col"),
        P(),
        P(),
        P(("groups", "frame"), "row", "col", None),
        P(),
        P(),
        P("row", "col"),
        P(),
        P(),
    )
    sizes = (mesh.shape["frame"], mesh.shape["row"], mesh.shape["col"])
    return jax.shard_map(
        functools.partial(per_device, sizes),
        mesh=mesh,
        in_specs=placed,
        out_specs=P(("groups", "row"), "col", "frame"),
        check_vma=False,
    )
```
